512 devices in a mesh: rep: 32 (over y_hi, z), fsdp: 16 (over y_lo, x, core).
Axes of the slice: x: 4, y: 4 (y_hi: 2, y_lo: 2; y = y_hi * 2 + y_lo), z: 16, core: 2. Of those that a mesh axis runs over, the one named last changes fastest.
Arguments:
- codes: int32 [32, 2, 32, 28672], P('rep', None, 'fsdp'), may hold values from -127 to 127
- scales: float32 [32, 2, 32], P('rep', None, 'fsdp'), may hold values from 0.004 to 0.04
- outer_params: float32 [2, 32, 28672], P(None, 'fsdp', 'rep'), may hold values from -6 to 6
- momentum: float32 [2, 32, 28672], P(None, 'fsdp', 'rep'), may hold values from -4 to 4
- local_params: bfloat16 [32, 2, 32, 28672], P('rep', None, 'fsdp'), may hold values from -6 to 6
- rates: float32 [32], replicated, may hold values from 0.35 to 1.4
- slot: int32 [32], replicated, may hold values from 0 to 31, each once
- tokens: bfloat16 [65536, 7168], P(('rep', 'fsdp')), may hold values from -6 to 6
- gain: bfloat16 [32, 7168], P('rep', 'fsdp'), may hold values from 0.5 to 1.5
- kv_weight: bfloat16 [32, 7168, 1024], P('rep', 'fsdp'), may hold values from -0.0625 to 0.0625
Outputs:
- keyvals: bfloat16 [65536, 1024], P(('rep', 'fsdp'))
- new_outer: float32 [2, 32, 28672], P(None, 'fsdp', 'rep')
- new_momentum: float32 [2, 32, 28672], P(None, 'fsdp', 'rep')
- blended: bfloat16 [32, 2, 32, 28672], P('rep', None, 'fsdp')
The draws below stay inside these ranges and needn't reach their ends.
Inputs may be any that keep to these rules, and one draw needn't show every extreme that they name: slot holds each of 0 to 31 once.
All inputs are finite; a program needn't handle non-finite values.
Results may differ from the reference program's by a relative error of at most 0.005.
Values may be sent and summed in bfloat16 or wider, within the bound.
A program may use at most 128 MiB of HBM per device.

```python
import math
import jax
import jax.numpy as jnp
from jax import lax

D = 7168
FF = 28672
LAYERS = 2
SLOTS = 32
TOK_DEV = 128
KVC = 1024
ROWS = 32
REPLICAS = 32
TOKENS = 65536
N_REP = 32
N_FSDP = 16


def plant(entries, key, low, top_value):
    index_at = [jax.random.randint(jax.random.fold_in(key, axis), (), 0, length) for axis, length in enumerate(entries.shape)]
    widest = entries.shape.index(max(entries.shape))
    neighbour = index_at[:widest] + [(index_at[widest] + 1) % entries.shape[widest]] + index_at[widest + 1:]
    return entries.at[tuple(index_at)].set(low).at[tuple(neighbour)].set(top_value)


def block_scale(stream_key, shape, cuts, smallest, top_value):
    level = 1.0
    for dim, shards_of in cuts:
        steps = jax.random.uniform(jax.random.fold_in(jax.random.fold_in(stream_key, 6), dim), (shards_of,), jnp.float32, smallest / len(cuts), top_value / len(cuts))
        level = level * jnp.repeat(jnp.exp(steps), shape[dim] // shards_of).reshape((-1,) + (1,) * (len(shape) - 1 - dim))
    return level


def normal_values(own_key, shape, spread, limit, split=(), kind=jnp.bfloat16):
    entries = jax.random.normal(own_key, shape, jnp.float32) * spread
    if len(split) > 0:
        entries = block_scale(own_key, shape, split, -0.22, 0.18) * entries
    return jnp.clip(entries, min=-limit, max=limit).astype(kind)


def setup_inputs(seed: int = 0) -> dict:
    streams_of = jax.random.split(jax.random.key(seed), 11)
    codes = plant(jax.random.randint(streams_of[0], (REPLICAS, LAYERS, ROWS, FF), -127, 128), jax.random.fold_in(streams_of[0], 1), -127, 127).astype(jnp.int32)
    scales = jnp.clip(jnp.exp(math.log(0.04) - 2.30258502 * jax.random.uniform(streams_of[1], (REPLICAS, LAYERS, ROWS), jnp.float32) ** block_scale(streams_of[1], (REPLICAS, LAYERS, ROWS), ((0, 32), (2, 16)), -0.2, 0.2)), 0.004, 0.04)
    outer_params = normal_values(streams_of[2], (LAYERS, ROWS, FF), 1.0, 6.0, ((1, 16), (2, 32)), jnp.float32)
    momentum = normal_values(streams_of[3], (LAYERS, ROWS, FF), 0.5, 4.0, ((1, 16), (2, 32)), jnp.float32)
    local_params = normal_values(streams_of[4], (REPLICAS, LAYERS, ROWS, FF), 1.0, 6.0, ((0, 32), (2, 16)))
    rates = jnp.clip(jnp.exp(jax.random.uniform(streams_of[5], (SLOTS,), jnp.float32, math.log(0.35), math.log(1.4))), 0.35, 1.4)
    slot = jax.random.permutation(streams_of[6], SLOTS).astype(jnp.int32)
    tokens = normal_values(streams_of[7], (TOKENS, D), 1.0, 6.0, ((0, 512),))
    gain = jnp.clip(1.0 + 0.1 * jax.random.normal(streams_of[8], (REPLICAS, D), jnp.float32), 0.5, 1.5).astype(jnp.bfloat16)
    kv_weight = normal_values(streams_of[9], (REPLICAS, D, KVC), D ** -0.5, 0.0625, ((0, 32), (1, 16)))
    return {"codes": codes, "scales": scales, "outer_params": outer_params, "momentum": momentum, "local_params": local_params, "rates": rates, "slot": slot, "tokens": tokens, "gain": gain, "kv_weight": kv_weight}


def project_replica(packed):
    block, gains, weights = packed
    values = block.astype(jnp.float32)
    inverse = lax.rsqrt(lax.optimization_barrier(jnp.mean(values * values, axis=1, keepdims=True)) + 1e-05)
    normed = (values * inverse * gains.astype(jnp.float32)).astype(jnp.bfloat16)
    return jnp.dot(normed, weights, preferred_element_type=jnp.float32).astype(jnp.bfloat16)

def reference(codes, scales, outer_params, momentum, local_params, rates, slot, tokens, gain, kv_weight):
    delta_sum = lax.optimization_barrier(jnp.sum(codes.astype(jnp.float32) * scales[..., None], axis=0))
    mean_delta = delta_sum / N_REP
    rate = rates[slot[0]]
    new_momentum = 0.9 * momentum + mean_delta
    new_outer = outer_params - rate * (mean_delta + 0.9 * new_momentum)
    blended = (0.5 * local_params.astype(jnp.float32) + 0.5 * new_outer[None]).astype(jnp.bfloat16)
    grouped = tokens.reshape(N_REP, TOK_DEV * N_FSDP, D)
    keyvals = lax.map(project_replica, (grouped, gain, kv_weight))
    return (keyvals.reshape(TOKENS, KVC), new_outer, new_momentum, blended)
```

```python
import functools

import jax
import jax.numpy as jnp
from jax import lax
from jax.experimental import pallas as pl
from jax.experimental.pallas import tpu as pltpu
from jax.sharding import PartitionSpec as P

F32 = jnp.float32
BF16 = jnp.bfloat16
CHUNKS = 4
NX = 4


def remote(src, dst, send, recv, device):
    return pltpu.make_async_remote_copy(
        src_ref=src,
        dst_ref=dst,
        send_sem=send,
        recv_sem=recv,
        device_id=device,
        device_id_type=pl.DeviceIdType.MESH,
    )


def kernel(
    nz,
    scales,
    rates,
    slot,
    gain,
    tokens,
    weight,
    codes,
    params,
    moment,
    local,
    keyvals_out,
    outer_out,
    moment_out,
    blended_out,
    tok,
    xs,
    relay,
    wraw,
    wk,
    own,
    held,
    c2_send,
    c2_recv,
    c1_send,
    c1_recv,
    kv,
    cb,
    stage_far,
    stage_own,
    fs,
    fr,
    msg,
    rb,
    total,
    pm,
    res,
    rc,
    blocks,
    lp,
    bl,
    load_sem,
    tok_sem,
    wload_sem,
    out_sem,
    xs_send,
    xs_recv,
    rl_send,
    rl_recv,
    fw_send,
    wy_send,
    wy_recv,
    wc_send,
    wc_recv,
    wf_send,
    wf_recv,
    c2s,
    c2r,
    c1s,
    c1r,
    za_send,
    za_recv,
    zb_send,
    zb_recv,
    ph_send,
    ph_recv,
    fb_send,
    fb_recv,
    here,
):
    count = tokens.shape[0]
    width = tokens.shape[1] // 8
    cols = res.shape[3]
    wide = msg.shape[2]
    runs = [(g, g * wide, min(wide, cols - g * wide)) for g in range(4) if g * wide < cols]
    part = kv.shape[1] // CHUNKS
    shard = weight.shape[1]

    me_r = lax.axis_index("rep")
    me_f = lax.axis_index("fsdp")
    z, yh = lax.rem(me_r, nz), lax.div(me_r, nz)
    core, x, y = lax.rem(me_f, 2), lax.rem(lax.div(me_f, 2), NX), lax.div(me_f, 2 * NX)

    def on_x(step):
        return (me_r, y * (2 * NX) + lax.rem(x + step, NX) * 2 + core)

    right, left = on_x(1), on_x(NX - 1)
    across = (me_r, (1 - y) * (2 * NX) + x * 2 + core)
    twin = (me_r, me_f + 1 - 2 * core)
    far = (lax.rem(me_r + nz, 2 * nz), me_f)

    def on_z(k):
        return (yh * nz + lax.rem(z + k, nz), me_f)

    def signal(sem, device):
        pl.semaphore_signal(sem, inc=1, device_id=device, device_id_type=pl.DeviceIdType.MESH)

    barrier = pltpu.get_barrier_semaphore()
    neighbours = (right, left, across, twin, far, on_z(1), on_z(nz - 1))
    for device in neighbours:
        signal(barrier, device)

    def piece(owner, rel):
        h = y if rel == 0 else 1 - y
        start = pl.multiple_of((h * NX + owner) * width, 128)
        return tokens.at[:, pl.ds(start, width)]

    load_codes = pltpu.make_async_copy(codes.at[0], cb, load_sem.at[0])
    wloads = [
        pltpu.make_async_copy(
            weight.at[0, :, pl.ds(n * part, part)], wraw.at[n], wload_sem.at[n]
        )
        for n in range(CHUNKS)
    ]
    load_tok = [
        [
            pltpu.make_async_copy(
                piece(lax.rem(x + d, NX), rel),
                tok.at[rel, d] if d else xs.at[rel, 0],
                tok_sem.at[rel, d],
            )
            for d in range(NX)
        ]
        for rel in range(2)
    ]
    load_pm = [
        pltpu.make_async_copy(ref, pm.at[i], load_sem.at[4 + i])
        for i, ref in enumerate((params, moment))
    ]
    load_lp = pltpu.make_async_copy(local.at[0], lp, load_sem.at[6])
    load_tok[0][2].start()
    load_tok[1][2].start()
    load_codes.start()
    for copy in wloads:
        copy.start()
    for rel, d in ((0, 1), (0, 3), (1, 1), (1, 3), (0, 0), (1, 0)):
        load_tok[rel][d].start()
    for copy in load_pm + [load_lp]:
        copy.start()
    for stage in (stage_far, stage_own):
        stage[...] = jnp.zeros(stage.shape, F32)

    load_codes.wait()
    row_at = lax.broadcasted_iota(jnp.int32, (2, 1), 0)

    def terms(stage, half_y):
        for l in range(2):
            row_scale = jnp.where(row_at == 0, scales[0, l, 0], scales[0, l, 1])
            for to in range(nz):
                for g, start, size in runs:
                    at = pl.multiple_of((half_y * nz + to) * cols + start, 128)
                    row = g * 4 + l * 2
                    stage[to, row : row + 2, :size] = (
                        cb[l, :, pl.ds(at, size)].astype(F32) * row_scale
                    )

    terms(stage_far, 1 - yh)
    for to in range(nz):
        fs[to] = stage_far[to].astype(BF16)
    halves = remote(fs, fr, ph_send.at[0], ph_recv.at[0], far)

    pl.semaphore_wait(barrier, len(neighbours))
    halves.start()

    def tell(turn):
        if 2 ** (turn + 1) < nz:
            for step in (2**turn, nz - 2**turn):
                signal(here.at[turn], on_z(step))

    def learn(turn):
        if 2 ** (turn + 1) < nz:
            pl.semaphore_wait(here.at[turn], 2)

    tell(0)

    relays = [
        remote(tok.at[0, 2], relay.at[0], rl_send.at[0], rl_recv.at[0], right),
        remote(tok.at[1, 2], relay.at[1], rl_send.at[1], rl_recv.at[1], left),
    ]
    forwards = [
        remote(relay.at[0], xs.at[0, 2], fw_send.at[0], xs_recv.at[0, 2], right),
        remote(relay.at[1], xs.at[1, 2], fw_send.at[1], xs_recv.at[1, 2], left),
    ]
    directs = [
        [
            remote(
                tok.at[rel, d],
                xs.at[rel, NX - d],
                xs_send.at[rel, NX - d],
                xs_recv.at[rel, NX - d],
                device,
            )
            for d, device in ((1, right), (3, left))
        ]
        for rel in range(2)
    ]
    for rel in range(2):
        load_tok[rel][2].wait()
        relays[rel].start()
    at_row = lax.broadcasted_iota(jnp.int32, (shard, shard), 0)
    at_col = lax.broadcasted_iota(jnp.int32, (shard, shard), 1)
    gain_col = jnp.sum(
        jnp.where(at_row == at_col, gain[...].astype(F32), 0.0), axis=1, keepdims=True
    )
    w_across = [
        remote(wk.at[n, 0, core], wk.at[n, 1, core], wy_send.at[n], wy_recv.at[n], across)
        for n in range(CHUNKS)
    ]
    w_twin = [
        remote(wk.at[n, 0, core], wk.at[n, 0, core], wc_send.at[n], wc_recv.at[n], twin)
        for n in range(CHUNKS)
    ]
    w_forward = [
        remote(wk.at[n, 1, core], wk.at[n, 1, core], wf_send.at[n], wf_recv.at[n], twin)
        for n in range(CHUNKS)
    ]

    def scale_chunk(n):
        wloads[n].wait()
        wk[n, 0, core] = (wraw[n].astype(F32) * gain_col).astype(BF16)
        w_across[n].start()
        w_twin[n].start()

    def send_direct(rel):
        for i, d in enumerate((1, 3)):
            load_tok[rel][d].wait()
            directs[rel][i].start()

    scale_chunk(0)
    send_direct(0)
    learn(0)
    tell(1)
    scale_chunk(1)
    terms(stage_own, yh)
    learn(1)
    tell(2)

    halves.wait_recv()
    for to in range(nz):
        stage_own[to] = stage_own[to] + fr[to].astype(F32)
        msg[to] = stage_own[to].astype(BF16)
    learn(2)

    def offset(i):
        return nz // 2 + (1 - 2 * lax.rem(i, 2)) * lax.div(i + 1, 2)

    def z_terms(k):
        return remote(msg.at[lax.rem(z + k, nz)], rb.at[k], za_send.at[k], za_recv.at[k], on_z(k))

    def send_terms(i, carry):
        z_terms(offset(i)).start()
        return carry

    lax.fori_loop(0, nz - 1, send_terms, 0)
    for rel in range(2):
        relays[rel].wait_recv()
        forwards[rel].start()
    send_direct(1)
    directs = directs[0] + directs[1]
    for n in range(2, CHUNKS):
        scale_chunk(n)

    squares = jnp.zeros((count, 1), F32)
    for rel in range(2):
        load_tok[rel][0].wait()
        for d in range(NX):
            block = (tok[rel, d] if d else xs[rel, 0]).astype(F32)
            squares += jnp.sum(block * block, axis=1, keepdims=True)
    inverse = lax.rsqrt(squares / tokens.shape[1] + 1e-05)

    def pass_on(n):
        w_across[n].wait_recv()
        w_forward[n].start()

    pass_on(0)

    def add_terms(k, total):
        z_terms(k).wait_recv()
        return total + rb[k].astype(F32)

    total[...] = lax.fori_loop(1, nz, add_terms, stage_own[z]) / (2 * nz)
    for copy in load_pm:
        copy.wait()
    rate = rates[slot[0]]
    for l in range(2):
        for g, start, size in runs:
            row = g * 4 + l * 2
            at = slice(start, start + size)
            mean_delta = total[row : row + 2, :size]
            new_moment = 0.9 * pm[1, l, :, at] + mean_delta
            new_outer = pm[0, l, :, at] - rate * (mean_delta + 0.9 * new_moment)
            res[0, l, :, at] = new_outer
            res[1, l, :, at] = new_moment
            total[row : row + 2, :size] = new_outer
    rc[yh, z] = total[...].astype(BF16)

    def z_outer(k, source):
        block = rc.at[yh, source]
        return remote(block, block, zb_send.at[k], zb_recv.at[source], on_z(k))

    def send_outer(i, carry):
        z_outer(offset(i), z).start()
        return carry

    lax.fori_loop(0, nz - 1, send_outer, 0)
    outs = [
        pltpu.make_async_copy(res.at[i], ref, out_sem.at[i])
        for i, ref in enumerate((outer_out, moment_out))
    ]
    for copy in outs:
        copy.start()

    pass_on(1)
    pass_on(2)
    for copy in directs + forwards:
        copy.wait_recv()

    sides = (right, left)
    c2 = [
        remote(c2_send.at[n], c2_recv.at[n], c2s.at[n], c2r.at[n], sides[n % 2])
        for n in range(CHUNKS)
    ]
    c1 = [
        [
            remote(c1_send.at[n, s], c1_recv.at[n, s], c1s.at[n, s], c1r.at[n, s], sides[s])
            for s in range(2)
        ]
        for n in range(CHUNKS)
    ]
    rows_of = {0: 1, 1: 3}

    def multiply(n):
        w_twin[n].wait_recv()
        w_forward[n].wait_recv()
        whole = sum(
            jnp.dot(
                xs[rel].reshape(NX * count, width),
                wk[n, rel].reshape(width, part),
                preferred_element_type=F32,
            )
            for rel in range(2)
        )

        def rows(d):
            return whole[d * count : (d + 1) * count]

        via, other = n % 2, 1 - n % 2
        c2_send[n] = rows(2).astype(BF16)
        c2[n].start()
        c1_send[n, other] = rows(rows_of[other]).astype(BF16)
        c1[n][other].start()
        held[n] = rows(rows_of[via])
        own[n] = rows(0)

    def combine(n):
        via = n % 2
        c2[n].wait_recv()
        c1_send[n, via] = (held[n] + c2_recv[n].astype(F32)).astype(BF16)
        c1[n][via].start()

    def finish(n):
        for s in range(2):
            c1[n][s].wait_recv()
        at = n * part
        whole = own[n] + c1_recv[n, 0].astype(F32) + c1_recv[n, 1].astype(F32)
        kv[:, at : at + part] = (whole * inverse).astype(BF16)

    multiply(0)
    multiply(1)
    combine(0)
    multiply(2)
    combine(1)
    pass_on(3)
    combine(2)
    multiply(3)

    def quarter(turn):
        return lax.rem(lax.div(z, 4) + turn, nz // 4)

    def hand_over(turn):
        block = rc.at[yh, pl.ds(quarter(turn) * 4, 4)]
        return remote(block, block, fb_send.at[turn], fb_recv.at[turn], far)

    for turn in range(nz // 4):
        for i in range(4):
            source = quarter(turn) * 4 + i

            @pl.when(source != z)
            def _():
                z_outer(0, source).wait_recv()

        hand_over(turn).start()
    combine(3)

    load_lp.wait()

    def blend(half_y, turn):
        for i in range(4):
            source = quarter(turn) * 4 + i
            blocks[i] = rc[half_y, source].astype(F32)
            for l in range(2):
                for g, start, size in runs:
                    row = g * 4 + l * 2
                    at = pl.ds(pl.multiple_of((half_y * nz + source) * cols + start, 128), size)
                    mine = lp[l, :, at].astype(F32)
                    new = blocks[i, row : row + 2, :size]
                    bl[l, :, at] = (0.5 * mine + 0.5 * new).astype(BF16)

    for turn in range(nz // 4):
        blend(yh, turn)
    for n in range(CHUNKS):
        finish(n)
    out_kv = pltpu.make_async_copy(kv, keyvals_out, out_sem.at[3])
    out_kv.start()
    for turn in range(nz // 4):
        hand_over(turn).wait_recv()
        blend(1 - yh, turn)
    out_blend = pltpu.make_async_copy(bl, blended_out.at[0], out_sem.at[2])
    out_blend.start()


    for copy in relays + directs + forwards + w_across + w_twin + w_forward + [halves] + c2:
        copy.wait_send()
    for turn in range(nz // 4):
        hand_over(turn).wait_send()
    for pair in c1:
        for copy in pair:
            copy.wait_send()

    def drain(k, carry):
        z_terms(k).wait_send()
        z_outer(k, z).wait_send()
        return carry

    lax.fori_loop(1, nz, drain, 0)
    for copy in outs + [out_blend, out_kv]:
        copy.wait()


def place(*refs):
    count = (len(refs) - 2) // 3
    sources, results, held = refs[:count], refs[count : 2 * count], refs[2 * count : 3 * count]
    into, out = refs[3 * count :]
    loads = [pltpu.make_async_copy(sources[i], held[i], into.at[i]) for i in range(count)]
    stores = [pltpu.make_async_copy(held[i], results[i], out.at[i]) for i in range(count)]
    for copy in loads:
        copy.start()
    for load, store in zip(loads, stores):
        load.wait()
        store.start()
    for copy in stores:
        copy.wait()


def shards(
    codes, scales, outer_params, momentum, local_params, rates, slot, tokens, gain, kv_weight
):
    nz = lax.axis_size("rep") // 2
    count, depth = tokens.shape
    width = depth // 8
    out_cols = kv_weight.shape[2]
    part = out_cols // CHUNKS
    shard = kv_weight.shape[1]
    full = codes.shape[3]
    cols = outer_params.shape[2]
    wide = (cols // 128 + 3) // 4 * 128
    dma = pltpu.SemaphoreType.DMA
    smem = pl.BlockSpec(memory_space=pltpu.SMEM)
    hbm = pl.BlockSpec(memory_space=pl.ANY)
    scratch = [
        pltpu.VMEM((2, NX, count, width), BF16),
        pltpu.VMEM((2, NX, count, width), BF16),
        pltpu.VMEM((2, count, width), BF16),
        pltpu.VMEM((CHUNKS, shard, part), BF16),
        pltpu.VMEM((CHUNKS, 2, 2, shard, part), BF16),
        pltpu.VMEM((CHUNKS, count, part), F32),
        pltpu.VMEM((CHUNKS, count, part), F32),
        pltpu.VMEM((CHUNKS, count, part), BF16),
        pltpu.VMEM((CHUNKS, count, part), BF16),
        pltpu.VMEM((CHUNKS, 2, count, part), BF16),
        pltpu.VMEM((CHUNKS, 2, count, part), BF16),
        pltpu.VMEM((count, out_cols), BF16),
        pltpu.VMEM((2, 2, full), jnp.int32),
        pltpu.VMEM((nz, 16, wide), F32),
        pltpu.VMEM((nz, 16, wide), F32),
        pltpu.VMEM((nz, 16, wide), BF16),
        pltpu.VMEM((nz, 16, wide), BF16),
        pltpu.VMEM((nz, 16, wide), BF16),
        pltpu.VMEM((nz, 16, wide), BF16),
        pltpu.VMEM((16, wide), F32),
        pltpu.VMEM((2, 2, 2, cols), F32),
        pltpu.VMEM((2, 2, 2, cols), F32),
        pltpu.VMEM((2, nz, 16, wide), BF16),
        pltpu.VMEM((4, 16, wide), F32),
        pltpu.VMEM((2, 2, full), BF16),
        pltpu.VMEM((2, 2, full), BF16),
        dma((7,)),
        dma((2, NX)),
        dma((CHUNKS,)),
        dma((4,)),
        dma((2, NX)),
        dma((2, NX)),
        dma((2,)),
        dma((2,)),
        dma((2,)),
        dma((CHUNKS,)),
        dma((CHUNKS,)),
        dma((CHUNKS,)),
        dma((CHUNKS,)),
        dma((CHUNKS,)),
        dma((CHUNKS,)),
        dma((CHUNKS,)),
        dma((CHUNKS,)),
        dma((CHUNKS, 2)),
        dma((CHUNKS, 2)),
        dma((nz,)),
        dma((nz,)),
        dma((nz,)),
        dma((nz,)),
        dma((1,)),
        dma((1,)),
        dma((4,)),
        dma((4,)),
        pltpu.SemaphoreType.REGULAR((4,)),
    ]
    results = pl.pallas_call(
        functools.partial(kernel, nz),
        out_shape=(
            jax.ShapeDtypeStruct((count, out_cols), BF16),
            jax.ShapeDtypeStruct(outer_params.shape, F32),
            jax.ShapeDtypeStruct(momentum.shape, F32),
            jax.ShapeDtypeStruct(local_params.shape, BF16),
        ),
        in_specs=[smem, smem, smem, pl.BlockSpec(memory_space=pltpu.VMEM)] + [hbm] * 6,
        out_specs=(hbm,) * 4,
        scratch_shapes=scratch,
        compiler_params=pltpu.CompilerParams(
            collective_id=0, has_side_effects=True, vmem_limit_bytes=60 * 2**20
        ),
        cost_estimate=pl.CostEstimate(
            flops=2 * count * depth * out_cols, bytes_accessed=8 * 2**20, transcendentals=count
        ),
    )(scales, rates, slot, gain, tokens, kv_weight, codes, outer_params, momentum, local_params)
    return pl.pallas_call(
        place,
        out_shape=tuple(jax.ShapeDtypeStruct(r.shape, r.dtype) for r in results),
        in_specs=[hbm] * len(results),
        out_specs=(hbm,) * len(results),
        scratch_shapes=[pltpu.VMEM(r.shape, r.dtype) for r in results]
        + [dma((len(results),))] * 2,
        compiler_params=pltpu.CompilerParams(vmem_limit_bytes=60 * 2**20),
    )(*results)


def solution(mesh):
    return jax.shard_map(
        shards,
        mesh=mesh,
        in_specs=(
            P("rep", None, "fsdp", None),
            P("rep", None, "fsdp"),
            P(None, "fsdp", "rep"),
            P(None, "fsdp", "rep"),
            P("rep", None, "fsdp", None),
            P(),
            P(),
            P(("rep", "fsdp"), None),
            P("rep", "fsdp"),
            P("rep", "fsdp", None),
        ),
        out_specs=(
            P(("rep", "fsdp"), None),
            P(None, "fsdp", "rep"),
            P(None, "fsdp", "rep"),
            P("rep", None, "fsdp", None),
        ),
        check_vma=False,
    )
```

```python
import functools

import jax
import jax.numpy as jnp
from jax import lax
from jax.experimental import pallas as pl
from jax.experimental.pallas import tpu as pltpu
from jax.sharding import PartitionSpec as P

F32 = jnp.float32
BF16 = jnp.bfloat16
CHUNKS = 4
NX = 4


def remote(src, dst, send, recv, device):
    return pltpu.make_async_remote_copy(
        src_ref=src,
        dst_ref=dst,
        send_sem=send,
        recv_sem=recv,
        device_id=device,
        device_id_type=pl.DeviceIdType.MESH,
    )


def kernel(
    nz,
    scales,
    rates,
    slot,
    gain,
    tokens,
    weight,
    codes,
    params,
    moment,
    local,
    keyvals_out,
    outer_out,
    moment_out,
    blended_out,
    tok,
    xs,
    relay,
    wraw,
    wk,
    own,
    held,
    c2_send,
    c2_recv,
    c1_send,
    c1_recv,
    kv,
    cb,
    stage_far,
    stage_own,
    fs,
    fr,
    msg,
    rb,
    total,
    pm,
    res,
    rc,
    blocks,
    lp,
    bl,
    load_sem,
    tok_sem,
    wload_sem,
    out_sem,
    xs_send,
    xs_recv,
    rl_send,
    rl_recv,
    fw_send,
    wy_send,
    wy_recv,
    wc_send,
    wc_recv,
    wf_send,
    wf_recv,
    c2s,
    c2r,
    c1s,
    c1r,
    za_send,
    za_recv,
    zb_send,
    zb_recv,
    ph_send,
    ph_recv,
    fb_send,
    fb_recv,
    here,
):
    count = tokens.shape[0]
    width = tokens.shape[1] // 8
    cols = res.shape[3]
    wide = msg.shape[2]
    runs = [(g, g * wide, min(wide, cols - g * wide)) for g in range(4) if g * wide < cols]
    part = kv.shape[1] // CHUNKS
    shard = weight.shape[1]

    me_r = lax.axis_index("rep")
    me_f = lax.axis_index("fsdp")
    z, yh = lax.rem(me_r, nz), lax.div(me_r, nz)
    core, x, y = lax.rem(me_f, 2), lax.rem(lax.div(me_f, 2), NX), lax.div(me_f, 2 * NX)

    def on_x(step):
        return (me_r, y * (2 * NX) + lax.rem(x + step, NX) * 2 + core)

    right, left = on_x(1), on_x(NX - 1)
    across = (me_r, (1 - y) * (2 * NX) + x * 2 + core)
    twin = (me_r, me_f + 1 - 2 * core)
    far = (lax.rem(me_r + nz, 2 * nz), me_f)

    def on_z(k):
        return (yh * nz + lax.rem(z + k, nz), me_f)

    def signal(sem, device):
        pl.semaphore_signal(sem, inc=1, device_id=device, device_id_type=pl.DeviceIdType.MESH)

    barrier = pltpu.get_barrier_semaphore()
    neighbours = (right, left, across, twin, far, on_z(1), on_z(nz - 1))
    for device in neighbours:
        signal(barrier, device)

    def piece(owner, rel):
        h = y if rel == 0 else 1 - y
        start = pl.multiple_of((h * NX + owner) * width, 128)
        return tokens.at[:, pl.ds(start, width)]

    load_codes = pltpu.make_async_copy(codes.at[0], cb, load_sem.at[0])
    wloads = [
        pltpu.make_async_copy(
            weight.at[0, :, pl.ds(n * part, part)], wraw.at[n], wload_sem.at[n]
        )
        for n in range(CHUNKS)
    ]
    load_tok = [
        [
            pltpu.make_async_copy(
                piece(lax.rem(x + d, NX), rel),
                tok.at[rel, d] if d else xs.at[rel, 0],
                tok_sem.at[rel, d],
            )
            for d in range(NX)
        ]
        for rel in range(2)
    ]
    load_pm = [
        pltpu.make_async_copy(ref, pm.at[i], load_sem.at[4 + i])
        for i, ref in enumerate((params, moment))
    ]
    load_lp = pltpu.make_async_copy(local.at[0], lp, load_sem.at[6])
    load_tok[0][2].start()
    load_tok[1][2].start()
    load_codes.start()
    for copy in wloads:
        copy.start()
    for rel, d in ((0, 1), (0, 3), (1, 1), (1, 3), (0, 0), (1, 0)):
        load_tok[rel][d].start()
    for copy in load_pm + [load_lp]:
        copy.start()
    for stage in (stage_far, stage_own):
        stage[...] = jnp.zeros(stage.shape, F32)

    load_codes.wait()
    row_at = lax.broadcasted_iota(jnp.int32, (2, 1), 0)

    def terms(stage, half_y):
        for l in range(2):
            row_scale = jnp.where(row_at == 0, scales[0, l, 0], scales[0, l, 1])
            for to in range(nz):
                for g, start, size in runs:
                    at = pl.multiple_of((half_y * nz + to) * cols + start, 128)
                    row = g * 4 + l * 2
                    stage[to, row : row + 2, :size] = (
                        cb[l, :, pl.ds(at, size)].astype(F32) * row_scale
                    )

    terms(stage_far, 1 - yh)
    for to in range(nz):
        fs[to] = stage_far[to].astype(BF16)
    halves = remote(fs, fr, ph_send.at[0], ph_recv.at[0], far)

    pl.semaphore_wait(barrier, len(neighbours))
    halves.start()

    def tell(turn):
        if 2 ** (turn + 1) < nz:
            for step in (2**turn, nz - 2**turn):
                signal(here.at[turn], on_z(step))

    def learn(turn):
        if 2 ** (turn + 1) < nz:
            pl.semaphore_wait(here.at[turn], 2)

    tell(0)

    relays = [
        remote(tok.at[0, 2], relay.at[0], rl_send.at[0], rl_recv.at[0], right),
        remote(tok.at[1, 2], relay.at[1], rl_send.at[1], rl_recv.at[1], left),
    ]
    forwards = [
        remote(relay.at[0], xs.at[0, 2], fw_send.at[0], xs_recv.at[0, 2], right),
        remote(relay.at[1], xs.at[1, 2], fw_send.at[1], xs_recv.at[1, 2], left),
    ]
    directs = [
        [
            remote(
                tok.at[rel, d],
                xs.at[rel, NX - d],
                xs_send.at[rel, NX - d],
                xs_recv.at[rel, NX - d],
                device,
            )
            for d, device in ((1, right), (3, left))
        ]
        for rel in range(2)
    ]
    for rel in range(2):
        load_tok[rel][2].wait()
        relays[rel].start()
    at_row = lax.broadcasted_iota(jnp.int32, (shard, shard), 0)
    at_col = lax.broadcasted_iota(jnp.int32, (shard, shard), 1)
    gain_col = jnp.sum(
        jnp.where(at_row == at_col, gain[...].astype(F32), 0.0), axis=1, keepdims=True
    )
    w_across = [
        remote(wk.at[n, 0, core], wk.at[n, 1, core], wy_send.at[n], wy_recv.at[n], across)
        for n in range(CHUNKS)
    ]
    w_twin = [
        remote(wk.at[n, 0, core], wk.at[n, 0, core], wc_send.at[n], wc_recv.at[n], twin)
        for n in range(CHUNKS)
    ]
    w_forward = [
        remote(wk.at[n, 1, core], wk.at[n, 1, core], wf_send.at[n], wf_recv.at[n], twin)
        for n in range(CHUNKS)
    ]

    def scale_chunk(n):
        wloads[n].wait()
        wk[n, 0, core] = (wraw[n].astype(F32) * gain_col).astype(BF16)
        w_across[n].start()
        w_twin[n].start()

    def send_direct(rel):
        for i, d in enumerate((1, 3)):
            load_tok[rel][d].wait()
            directs[rel][i].start()

    scale_chunk(0)
    send_direct(0)
    learn(0)
    tell(1)
    scale_chunk(1)
    terms(stage_own, yh)
    scale_chunk(2)
    scale_chunk(3)
    learn(1)
    tell(2)

    halves.wait_recv()
    for to in range(nz):
        stage_own[to] = stage_own[to] + fr[to].astype(F32)
        msg[to] = stage_own[to].astype(BF16)
    learn(2)

    def offset(i):
        return nz // 2 + (1 - 2 * lax.rem(i, 2)) * lax.div(i + 1, 2)

    def z_terms(k):
        return remote(msg.at[lax.rem(z + k, nz)], rb.at[k], za_send.at[k], za_recv.at[k], on_z(k))

    def send_terms(i, carry):
        z_terms(offset(i)).start()
        return carry

    lax.fori_loop(0, nz - 1, send_terms, 0)
    for rel in range(2):
        relays[rel].wait_recv()
        forwards[rel].start()
    send_direct(1)
    directs = directs[0] + directs[1]

    squares = jnp.zeros((count, 1), F32)
    for rel in range(2):
        load_tok[rel][0].wait()
        for d in range(NX):
            block = (tok[rel, d] if d else xs[rel, 0]).astype(F32)
            squares += jnp.sum(block * block, axis=1, keepdims=True)
    inverse = lax.rsqrt(squares / tokens.shape[1] + 1e-05)

    def pass_on(n):
        w_across[n].wait_recv()
        w_forward[n].start()

    pass_on(0)

    def add_terms(k, total):
        z_terms(k).wait_recv()
        return total + rb[k].astype(F32)

    total[...] = lax.fori_loop(1, nz, add_terms, stage_own[z]) / (2 * nz)
    for copy in load_pm:
        copy.wait()
    rate = rates[slot[0]]
    for l in range(2):
        for g, start, size in runs:
            row = g * 4 + l * 2
            at = slice(start, start + size)
            mean_delta = total[row : row + 2, :size]
            new_moment = 0.9 * pm[1, l, :, at] + mean_delta
            new_outer = pm[0, l, :, at] - rate * (mean_delta + 0.9 * new_moment)
            res[0, l, :, at] = new_outer
            res[1, l, :, at] = new_moment
            total[row : row + 2, :size] = new_outer
    rc[yh, z] = total[...].astype(BF16)

    def z_outer(k, source):
        block = rc.at[yh, source]
        return remote(block, block, zb_send.at[k], zb_recv.at[source], on_z(k))

    def send_outer(i, carry):
        z_outer(offset(i), z).start()
        return carry

    lax.fori_loop(0, nz - 1, send_outer, 0)
    outs = [
        pltpu.make_async_copy(res.at[i], ref, out_sem.at[i])
        for i, ref in enumerate((outer_out, moment_out))
    ]
    for copy in outs:
        copy.start()

    pass_on(1)
    pass_on(2)
    for copy in directs + forwards:
        copy.wait_recv()

    sides = (right, left)
    c2 = [
        remote(c2_send.at[n], c2_recv.at[n], c2s.at[n], c2r.at[n], sides[n % 2])
        for n in range(CHUNKS)
    ]
    c1 = [
        [
            remote(c1_send.at[n, s], c1_recv.at[n, s], c1s.at[n, s], c1r.at[n, s], sides[s])
            for s in range(2)
        ]
        for n in range(CHUNKS)
    ]
    rows_of = {0: 1, 1: 3}

    def multiply(n):
        w_twin[n].wait_recv()
        w_forward[n].wait_recv()
        whole = sum(
            jnp.dot(
                xs[rel].reshape(NX * count, width),
                wk[n, rel].reshape(width, part),
                preferred_element_type=F32,
            )
            for rel in range(2)
        )

        def rows(d):
            return whole[d * count : (d + 1) * count]

        via, other = n % 2, 1 - n % 2
        c2_send[n] = rows(2).astype(BF16)
        c2[n].start()
        c1_send[n, other] = rows(rows_of[other]).astype(BF16)
        c1[n][other].start()
        held[n] = rows(rows_of[via])
        own[n] = rows(0)

    def combine(n):
        via = n % 2
        c2[n].wait_recv()
        c1_send[n, via] = (held[n] + c2_recv[n].astype(F32)).astype(BF16)
        c1[n][via].start()

    def finish(n):
        for s in range(2):
            c1[n][s].wait_recv()
        at = n * part
        whole = own[n] + c1_recv[n, 0].astype(F32) + c1_recv[n, 1].astype(F32)
        kv[:, at : at + part] = (whole * inverse).astype(BF16)

    multiply(0)
    multiply(1)
    combine(0)
    multiply(2)
    combine(1)
    pass_on(3)
    combine(2)
    multiply(3)

    def quarter(turn):
        return lax.rem(lax.div(z, 4) + turn, nz // 4)

    def hand_over(turn):
        block = rc.at[yh, pl.ds(quarter(turn) * 4, 4)]
        return remote(block, block, fb_send.at[turn], fb_recv.at[turn], far)

    for turn in range(nz // 4):
        for i in range(4):
            source = quarter(turn) * 4 + i

            @pl.when(source != z)
            def _():
                z_outer(0, source).wait_recv()

        hand_over(turn).start()
    combine(3)

    load_lp.wait()

    def blend(half_y, turn):
        for i in range(4):
            source = quarter(turn) * 4 + i
            blocks[i] = rc[half_y, source].astype(F32)
            for l in range(2):
                for g, start, size in runs:
                    row = g * 4 + l * 2
                    at = pl.ds(pl.multiple_of((half_y * nz + source) * cols + start, 128), size)
                    mine = lp[l, :, at].astype(F32)
                    new = blocks[i, row : row + 2, :size]
                    bl[l, :, at] = (0.5 * mine + 0.5 * new).astype(BF16)

    def write_half(half_y, sem):
        at = pl.ds(pl.multiple_of(half_y * nz * cols, 128), nz * cols)
        copy = pltpu.make_async_copy(bl.at[:, :, at], blended_out.at[0, :, :, at], sem)
        copy.start()
        return copy

    for turn in range(nz // 4):
        blend(yh, turn)
    out_near = write_half(yh, out_sem.at[2])
    for n in range(CHUNKS):
        finish(n)
    out_kv = pltpu.make_async_copy(kv, keyvals_out, out_sem.at[3])
    out_kv.start()
    for turn in range(nz // 4):
        hand_over(turn).wait_recv()
        blend(1 - yh, turn)
    out_far = write_half(1 - yh, out_sem.at[4])


    for copy in relays + directs + forwards + w_across + w_twin + w_forward + [halves] + c2:
        copy.wait_send()
    for turn in range(nz // 4):
        hand_over(turn).wait_send()
    for pair in c1:
        for copy in pair:
            copy.wait_send()

    def drain(k, carry):
        z_terms(k).wait_send()
        z_outer(k, z).wait_send()
        return carry

    lax.fori_loop(1, nz, drain, 0)
    for copy in outs + [out_near, out_far, out_kv]:
        copy.wait()


def place(*refs):
    count = (len(refs) - 2) // 3
    sources, results, held = refs[:count], refs[count : 2 * count], refs[2 * count : 3 * count]
    into, out = refs[3 * count :]
    loads = [pltpu.make_async_copy(sources[i], held[i], into.at[i]) for i in range(count)]
    stores = [pltpu.make_async_copy(held[i], results[i], out.at[i]) for i in range(count)]
    for copy in loads:
        copy.start()
    for load, store in zip(loads, stores):
        load.wait()
        store.start()
    for copy in stores:
        copy.wait()


def shards(
    codes, scales, outer_params, momentum, local_params, rates, slot, tokens, gain, kv_weight
):
    nz = lax.axis_size("rep") // 2
    count, depth = tokens.shape
    width = depth // 8
    out_cols = kv_weight.shape[2]
    part = out_cols // CHUNKS
    shard = kv_weight.shape[1]
    full = codes.shape[3]
    cols = outer_params.shape[2]
    wide = (cols // 128 + 3) // 4 * 128
    dma = pltpu.SemaphoreType.DMA
    smem = pl.BlockSpec(memory_space=pltpu.SMEM)
    hbm = pl.BlockSpec(memory_space=pl.ANY)
    scratch = [
        pltpu.VMEM((2, NX, count, width), BF16),
        pltpu.VMEM((2, NX, count, width), BF16),
        pltpu.VMEM((2, count, width), BF16),
        pltpu.VMEM((CHUNKS, shard, part), BF16),
        pltpu.VMEM((CHUNKS, 2, 2, shard, part), BF16),
        pltpu.VMEM((CHUNKS, count, part), F32),
        pltpu.VMEM((CHUNKS, count, part), F32),
        pltpu.VMEM((CHUNKS, count, part), BF16),
        pltpu.VMEM((CHUNKS, count, part), BF16),
        pltpu.VMEM((CHUNKS, 2, count, part), BF16),
        pltpu.VMEM((CHUNKS, 2, count, part), BF16),
        pltpu.VMEM((count, out_cols), BF16),
        pltpu.VMEM((2, 2, full), jnp.int32),
        pltpu.VMEM((nz, 16, wide), F32),
        pltpu.VMEM((nz, 16, wide), F32),
        pltpu.VMEM((nz, 16, wide), BF16),
        pltpu.VMEM((nz, 16, wide), BF16),
        pltpu.VMEM((nz, 16, wide), BF16),
        pltpu.VMEM((nz, 16, wide), BF16),
        pltpu.VMEM((16, wide), F32),
        pltpu.VMEM((2, 2, 2, cols), F32),
        pltpu.VMEM((2, 2, 2, cols), F32),
        pltpu.VMEM((2, nz, 16, wide), BF16),
        pltpu.VMEM((4, 16, wide), F32),
        pltpu.VMEM((2, 2, full), BF16),
        pltpu.VMEM((2, 2, full), BF16),
        dma((7,)),
        dma((2, NX)),
        dma((CHUNKS,)),
        dma((5,)),
        dma((2, NX)),
        dma((2, NX)),
        dma((2,)),
        dma((2,)),
        dma((2,)),
        dma((CHUNKS,)),
        dma((CHUNKS,)),
        dma((CHUNKS,)),
        dma((CHUNKS,)),
        dma((CHUNKS,)),
        dma((CHUNKS,)),
        dma((CHUNKS,)),
        dma((CHUNKS,)),
        dma((CHUNKS, 2)),
        dma((CHUNKS, 2)),
        dma((nz,)),
        dma((nz,)),
        dma((nz,)),
        dma((nz,)),
        dma((1,)),
        dma((1,)),
        dma((4,)),
        dma((4,)),
        pltpu.SemaphoreType.REGULAR((4,)),
    ]
    results = pl.pallas_call(
        functools.partial(kernel, nz),
        out_shape=(
            jax.ShapeDtypeStruct((count, out_cols), BF16),
            jax.ShapeDtypeStruct(outer_params.shape, F32),
            jax.ShapeDtypeStruct(momentum.shape, F32),
            jax.ShapeDtypeStruct(local_params.shape, BF16),
        ),
        in_specs=[smem, smem, smem, pl.BlockSpec(memory_space=pltpu.VMEM)] + [hbm] * 6,
        out_specs=(hbm,) * 4,
        scratch_shapes=scratch,
        compiler_params=pltpu.CompilerParams(
            collective_id=0, has_side_effects=True, vmem_limit_bytes=60 * 2**20
        ),
        cost_estimate=pl.CostEstimate(
            flops=2 * count * depth * out_cols, bytes_accessed=8 * 2**20, transcendentals=count
        ),
    )(scales, rates, slot, gain, tokens, kv_weight, codes, outer_params, momentum, local_params)
    return pl.pallas_call(
        place,
        out_shape=tuple(jax.ShapeDtypeStruct(r.shape, r.dtype) for r in results),
        in_specs=[hbm] * len(results),
        out_specs=(hbm,) * len(results),
        scratch_shapes=[pltpu.VMEM(r.shape, r.dtype) for r in results]
        + [dma((len(results),))] * 2,
        compiler_params=pltpu.CompilerParams(vmem_limit_bytes=60 * 2**20),
    )(*results)


def solution(mesh):
    return jax.shard_map(
        shards,
        mesh=mesh,
        in_specs=(
            P("rep", None, "fsdp", None),
            P("rep", None, "fsdp"),
            P(None, "fsdp", "rep"),
            P(None, "fsdp", "rep"),
            P("rep", None, "fsdp", None),
            P(),
            P(),
            P(("rep", "fsdp"), None),
            P("rep", "fsdp"),
            P("rep", "fsdp", None),
        ),
        out_specs=(
            P(("rep", "fsdp"), None),
            P(None, "fsdp", "rep"),
            P(None, "fsdp", "rep"),
            P("rep", None, "fsdp", None),
        ),
        check_vma=False,
    )
```

```python
import functools

import jax
import jax.numpy as jnp
from jax import lax
from jax.experimental import pallas as pl
from jax.experimental.pallas import tpu as pltpu
from jax.sharding import PartitionSpec as P

F32 = jnp.float32
BF16 = jnp.bfloat16
CHUNKS = 4
NX = 4


def remote(src, dst, send, recv, device):
    return pltpu.make_async_remote_copy(
        src_ref=src,
        dst_ref=dst,
        send_sem=send,
        recv_sem=recv,
        device_id=device,
        device_id_type=pl.DeviceIdType.MESH,
    )


def kernel(
    nz,
    scales,
    rates,
    slot,
    gain,
    tokens,
    weight,
    codes,
    params,
    moment,
    local,
    keyvals_out,
    outer_out,
    moment_out,
    blended_out,
    tok,
    xs,
    relay,
    wraw,
    wk,
    own,
    held,
    c2_send,
    c2_recv,
    c1_send,
    c1_recv,
    kv,
    cb,
    stage_far,
    stage_own,
    fs,
    fr,
    msg,
    rb,
    total,
    pm,
    res,
    rc,
    blocks,
    lp,
    bl,
    load_sem,
    tok_sem,
    wload_sem,
    out_sem,
    xs_send,
    xs_recv,
    rl_send,
    rl_recv,
    fw_send,
    wy_send,
    wy_recv,
    wc_send,
    wc_recv,
    wf_send,
    wf_recv,
    c2s,
    c2r,
    c1s,
    c1r,
    za_send,
    za_recv,
    zb_send,
    zb_recv,
    ph_send,
    ph_recv,
    fb_send,
    fb_recv,
    here,
):
    count = tokens.shape[0]
    width = tokens.shape[1] // 8
    cols = res.shape[3]
    wide = msg.shape[2]
    runs = [(g, g * wide, min(wide, cols - g * wide)) for g in range(4) if g * wide < cols]
    part = kv.shape[1] // CHUNKS
    shard = weight.shape[1]

    me_r = lax.axis_index("rep")
    me_f = lax.axis_index("fsdp")
    z, yh = lax.rem(me_r, nz), lax.div(me_r, nz)
    core, x, y = lax.rem(me_f, 2), lax.rem(lax.div(me_f, 2), NX), lax.div(me_f, 2 * NX)

    def on_x(step):
        return (me_r, y * (2 * NX) + lax.rem(x + step, NX) * 2 + core)

    right, left = on_x(1), on_x(NX - 1)
    across = (me_r, (1 - y) * (2 * NX) + x * 2 + core)
    twin = (me_r, me_f + 1 - 2 * core)
    far = (lax.rem(me_r + nz, 2 * nz), me_f)

    def on_z(k):
        return (yh * nz + lax.rem(z + k, nz), me_f)

    def signal(sem, device):
        pl.semaphore_signal(sem, inc=1, device_id=device, device_id_type=pl.DeviceIdType.MESH)

    barrier = pltpu.get_barrier_semaphore()
    neighbours = (right, left, across, twin, far, on_z(1), on_z(nz - 1))
    for device in neighbours:
        signal(barrier, device)

    def piece(owner, rel):
        h = y if rel == 0 else 1 - y
        start = pl.multiple_of((h * NX + owner) * width, 128)
        return tokens.at[:, pl.ds(start, width)]

    load_codes = pltpu.make_async_copy(codes.at[0], cb, load_sem.at[0])
    wloads = [
        pltpu.make_async_copy(
            weight.at[0, :, pl.ds(n * part, part)], wraw.at[n], wload_sem.at[n]
        )
        for n in range(CHUNKS)
    ]
    load_tok = [
        [
            pltpu.make_async_copy(
                piece(lax.rem(x + d, NX), rel),
                tok.at[rel, d] if d else xs.at[rel, 0],
                tok_sem.at[rel, d],
            )
            for d in range(NX)
        ]
        for rel in range(2)
    ]
    load_pm = [
        pltpu.make_async_copy(ref, pm.at[i], load_sem.at[4 + i])
        for i, ref in enumerate((params, moment))
    ]
    load_lp = pltpu.make_async_copy(local.at[0], lp, load_sem.at[6])
    load_tok[0][2].start()
    load_tok[1][2].start()
    load_codes.start()
    for copy in wloads:
        copy.start()
    for rel, d in ((0, 1), (0, 3), (1, 1), (1, 3), (0, 0), (1, 0)):
        load_tok[rel][d].start()
    for copy in load_pm + [load_lp]:
        copy.start()
    for stage in (stage_far, stage_own):
        stage[...] = jnp.zeros(stage.shape, F32)

    load_codes.wait()
    row_at = lax.broadcasted_iota(jnp.int32, (2, 1), 0)

    def terms(stage, half_y):
        for l in range(2):
            row_scale = jnp.where(row_at == 0, scales[0, l, 0], scales[0, l, 1])
            for to in range(nz):
                for g, start, size in runs:
                    at = pl.multiple_of((half_y * nz + to) * cols + start, 128)
                    row = g * 4 + l * 2
                    stage[to, row : row + 2, :size] = (
                        cb[l, :, pl.ds(at, size)].astype(F32) * row_scale
                    )

    terms(stage_far, 1 - yh)
    for to in range(nz):
        fs[to] = stage_far[to].astype(BF16)
    halves = remote(fs, fr, ph_send.at[0], ph_recv.at[0], far)

    pl.semaphore_wait(barrier, len(neighbours))
    halves.start()

    def tell(turn):
        if 2 ** (turn + 1) < nz:
            for step in (2**turn, nz - 2**turn):
                signal(here.at[turn], on_z(step))

    def learn(turn):
        if 2 ** (turn + 1) < nz:
            pl.semaphore_wait(here.at[turn], 2)

    tell(0)

    relays = [
        remote(tok.at[0, 2], relay.at[0], rl_send.at[0], rl_recv.at[0], right),
        remote(tok.at[1, 2], relay.at[1], rl_send.at[1], rl_recv.at[1], left),
    ]
    forwards = [
        remote(relay.at[0], xs.at[0, 2], fw_send.at[0], xs_recv.at[0, 2], right),
        remote(relay.at[1], xs.at[1, 2], fw_send.at[1], xs_recv.at[1, 2], left),
    ]
    directs = [
        [
            remote(
                tok.at[rel, d],
                xs.at[rel, NX - d],
                xs_send.at[rel, NX - d],
                xs_recv.at[rel, NX - d],
                device,
            )
            for d, device in ((1, right), (3, left))
        ]
        for rel in range(2)
    ]
    for rel in range(2):
        load_tok[rel][2].wait()
        relays[rel].start()
    at_row = lax.broadcasted_iota(jnp.int32, (shard, shard), 0)
    at_col = lax.broadcasted_iota(jnp.int32, (shard, shard), 1)
    gain_col = jnp.sum(
        jnp.where(at_row == at_col, gain[...].astype(F32), 0.0), axis=1, keepdims=True
    )
    w_across = [
        remote(wk.at[n, 0, core], wk.at[n, 1, core], wy_send.at[n], wy_recv.at[n], across)
        for n in range(CHUNKS)
    ]
    w_twin = [
        remote(wk.at[n, 0, core], wk.at[n, 0, core], wc_send.at[n], wc_recv.at[n], twin)
        for n in range(CHUNKS)
    ]
    w_forward = [
        remote(wk.at[n, 1, core], wk.at[n, 1, core], wf_send.at[n], wf_recv.at[n], twin)
        for n in range(CHUNKS)
    ]

    def scale_chunk(n):
        wloads[n].wait()
        wk[n, 0, core] = (wraw[n].astype(F32) * gain_col).astype(BF16)
        w_across[n].start()
        w_twin[n].start()

    def send_direct(rel):
        for i, d in enumerate((1, 3)):
            load_tok[rel][d].wait()
            directs[rel][i].start()

    scale_chunk(0)
    learn(0)
    tell(1)
    send_direct(0)
    scale_chunk(1)
    learn(1)
    tell(2)
    terms(stage_own, yh)

    halves.wait_recv()
    for to in range(nz):
        stage_own[to] = stage_own[to] + fr[to].astype(F32)
        msg[to] = stage_own[to].astype(BF16)
    learn(2)

    def offset(i):
        return nz // 2 + (1 - 2 * lax.rem(i, 2)) * lax.div(i + 1, 2)

    def z_terms(k):
        return remote(msg.at[lax.rem(z + k, nz)], rb.at[k], za_send.at[k], za_recv.at[k], on_z(k))

    def send_terms(i, carry):
        z_terms(offset(i)).start()
        return carry

    lax.fori_loop(0, nz - 1, send_terms, 0)
    scale_chunk(2)
    scale_chunk(3)
    for rel in range(2):
        relays[rel].wait_recv()
        forwards[rel].start()
    send_direct(1)
    directs = directs[0] + directs[1]

    squares = jnp.zeros((count, 1), F32)
    for rel in range(2):
        load_tok[rel][0].wait()
        for d in range(NX):
            block = (tok[rel, d] if d else xs[rel, 0]).astype(F32)
            squares += jnp.sum(block * block, axis=1, keepdims=True)
    inverse = lax.rsqrt(squares / tokens.shape[1] + 1e-05)

    def pass_on(n):
        w_across[n].wait_recv()
        w_forward[n].start()

    def add_terms(k, total):
        z_terms(k).wait_recv()
        return total + rb[k].astype(F32)

    total[...] = lax.fori_loop(1, nz, add_terms, stage_own[z]) / (2 * nz)
    for copy in load_pm:
        copy.wait()
    rate = rates[slot[0]]
    for l in range(2):
        for g, start, size in runs:
            row = g * 4 + l * 2
            at = slice(start, start + size)
            mean_delta = total[row : row + 2, :size]
            new_moment = 0.9 * pm[1, l, :, at] + mean_delta
            new_outer = pm[0, l, :, at] - rate * (mean_delta + 0.9 * new_moment)
            res[0, l, :, at] = new_outer
            res[1, l, :, at] = new_moment
            total[row : row + 2, :size] = new_outer
    rc[yh, z] = total[...].astype(BF16)

    def z_outer(k, source):
        block = rc.at[yh, source]
        return remote(block, block, zb_send.at[k], zb_recv.at[source], on_z(k))

    def send_outer(i, carry):
        z_outer(offset(i), z).start()
        return carry

    lax.fori_loop(0, nz - 1, send_outer, 0)
    outs = [
        pltpu.make_async_copy(res.at[i], ref, out_sem.at[i])
        for i, ref in enumerate((outer_out, moment_out))
    ]
    for copy in outs:
        copy.start()

    pass_on(0)
    pass_on(1)
    pass_on(2)
    for copy in directs + forwards:
        copy.wait_recv()

    sides = (right, left)
    c2 = [
        remote(c2_send.at[n], c2_recv.at[n], c2s.at[n], c2r.at[n], sides[n % 2])
        for n in range(CHUNKS)
    ]
    c1 = [
        [
            remote(c1_send.at[n, s], c1_recv.at[n, s], c1s.at[n, s], c1r.at[n, s], sides[s])
            for s in range(2)
        ]
        for n in range(CHUNKS)
    ]
    rows_of = {0: 1, 1: 3}

    def multiply(n):
        w_twin[n].wait_recv()
        w_forward[n].wait_recv()
        whole = sum(
            jnp.dot(
                xs[rel].reshape(NX * count, width),
                wk[n, rel].reshape(width, part),
                preferred_element_type=F32,
            )
            for rel in range(2)
        )

        def rows(d):
            return whole[d * count : (d + 1) * count]

        via, other = n % 2, 1 - n % 2
        c2_send[n] = rows(2).astype(BF16)
        c2[n].start()
        c1_send[n, other] = rows(rows_of[other]).astype(BF16)
        c1[n][other].start()
        held[n] = rows(rows_of[via])
        own[n] = rows(0)

    def combine(n):
        via = n % 2
        c2[n].wait_recv()
        c1_send[n, via] = (held[n] + c2_recv[n].astype(F32)).astype(BF16)
        c1[n][via].start()

    def finish(n):
        for s in range(2):
            c1[n][s].wait_recv()
        at = n * part
        whole = own[n] + c1_recv[n, 0].astype(F32) + c1_recv[n, 1].astype(F32)
        kv[:, at : at + part] = (whole * inverse).astype(BF16)

    multiply(0)
    multiply(1)
    combine(0)
    multiply(2)
    combine(1)
    pass_on(3)
    combine(2)
    multiply(3)

    def quarter(turn):
        return lax.rem(lax.div(z, 4) + turn, nz // 4)

    def hand_over(turn):
        block = rc.at[yh, pl.ds(quarter(turn) * 4, 4)]
        return remote(block, block, fb_send.at[turn], fb_recv.at[turn], far)

    for turn in range(nz // 4):
        for i in range(4):
            source = quarter(turn) * 4 + i

            @pl.when(source != z)
            def _():
                z_outer(0, source).wait_recv()

        hand_over(turn).start()
    combine(3)

    load_lp.wait()

    def blend(half_y, turn):
        for i in range(4):
            source = quarter(turn) * 4 + i
            blocks[i] = rc[half_y, source].astype(F32)
            for l in range(2):
                for g, start, size in runs:
                    row = g * 4 + l * 2
                    at = pl.ds(pl.multiple_of((half_y * nz + source) * cols + start, 128), size)
                    mine = lp[l, :, at].astype(F32)
                    new = blocks[i, row : row + 2, :size]
                    bl[l, :, at] = (0.5 * mine + 0.5 * new).astype(BF16)

    def write_half(half_y, sem):
        at = pl.ds(pl.multiple_of(half_y * nz * cols, 128), nz * cols)
        copy = pltpu.make_async_copy(bl.at[:, :, at], blended_out.at[0, :, :, at], sem)
        copy.start()
        return copy

    for turn in range(nz // 4):
        blend(yh, turn)
    out_near = write_half(yh, out_sem.at[2])
    for n in range(CHUNKS):
        finish(n)
    out_kv = pltpu.make_async_copy(kv, keyvals_out, out_sem.at[3])
    out_kv.start()
    for turn in range(nz // 4):
        hand_over(turn).wait_recv()
        blend(1 - yh, turn)
    out_far = write_half(1 - yh, out_sem.at[4])


    for copy in relays + directs + forwards + w_across + w_twin + w_forward + [halves] + c2:
        copy.wait_send()
    for turn in range(nz // 4):
        hand_over(turn).wait_send()
    for pair in c1:
        for copy in pair:
            copy.wait_send()

    def drain(k, carry):
        z_terms(k).wait_send()
        z_outer(k, z).wait_send()
        return carry

    lax.fori_loop(1, nz, drain, 0)
    for copy in outs + [out_near, out_far, out_kv]:
        copy.wait()


def place(*refs):
    count = (len(refs) - 2) // 3
    sources, results, held = refs[:count], refs[count : 2 * count], refs[2 * count : 3 * count]
    into, out = refs[3 * count :]
    loads = [pltpu.make_async_copy(sources[i], held[i], into.at[i]) for i in range(count)]
    stores = [pltpu.make_async_copy(held[i], results[i], out.at[i]) for i in range(count)]
    for copy in loads:
        copy.start()
    for load, store in zip(loads, stores):
        load.wait()
        store.start()
    for copy in stores:
        copy.wait()


def shards(
    codes, scales, outer_params, momentum, local_params, rates, slot, tokens, gain, kv_weight
):
    nz = lax.axis_size("rep") // 2
    count, depth = tokens.shape
    width = depth // 8
    out_cols = kv_weight.shape[2]
    part = out_cols // CHUNKS
    shard = kv_weight.shape[1]
    full = codes.shape[3]
    cols = outer_params.shape[2]
    wide = (cols // 128 + 3) // 4 * 128
    dma = pltpu.SemaphoreType.DMA
    smem = pl.BlockSpec(memory_space=pltpu.SMEM)
    hbm = pl.BlockSpec(memory_space=pl.ANY)
    scratch = [
        pltpu.VMEM((2, NX, count, width), BF16),
        pltpu.VMEM((2, NX, count, width), BF16),
        pltpu.VMEM((2, count, width), BF16),
        pltpu.VMEM((CHUNKS, shard, part), BF16),
        pltpu.VMEM((CHUNKS, 2, 2, shard, part), BF16),
        pltpu.VMEM((CHUNKS, count, part), F32),
        pltpu.VMEM((CHUNKS, count, part), F32),
        pltpu.VMEM((CHUNKS, count, part), BF16),
        pltpu.VMEM((CHUNKS, count, part), BF16),
        pltpu.VMEM((CHUNKS, 2, count, part), BF16),
        pltpu.VMEM((CHUNKS, 2, count, part), BF16),
        pltpu.VMEM((count, out_cols), BF16),
        pltpu.VMEM((2, 2, full), jnp.int32),
        pltpu.VMEM((nz, 16, wide), F32),
        pltpu.VMEM((nz, 16, wide), F32),
        pltpu.VMEM((nz, 16, wide), BF16),
        pltpu.VMEM((nz, 16, wide), BF16),
        pltpu.VMEM((nz, 16, wide), BF16),
        pltpu.VMEM((nz, 16, wide), BF16),
        pltpu.VMEM((16, wide), F32),
        pltpu.VMEM((2, 2, 2, cols), F32),
        pltpu.VMEM((2, 2, 2, cols), F32),
        pltpu.VMEM((2, nz, 16, wide), BF16),
        pltpu.VMEM((4, 16, wide), F32),
        pltpu.VMEM((2, 2, full), BF16),
        pltpu.VMEM((2, 2, full), BF16),
        dma((7,)),
        dma((2, NX)),
        dma((CHUNKS,)),
        dma((5,)),
        dma((2, NX)),
        dma((2, NX)),
        dma((2,)),
        dma((2,)),
        dma((2,)),
        dma((CHUNKS,)),
        dma((CHUNKS,)),
        dma((CHUNKS,)),
        dma((CHUNKS,)),
        dma((CHUNKS,)),
        dma((CHUNKS,)),
        dma((CHUNKS,)),
        dma((CHUNKS,)),
        dma((CHUNKS, 2)),
        dma((CHUNKS, 2)),
        dma((nz,)),
        dma((nz,)),
        dma((nz,)),
        dma((nz,)),
        dma((1,)),
        dma((1,)),
        dma((4,)),
        dma((4,)),
        pltpu.SemaphoreType.REGULAR((4,)),
    ]
    results = pl.pallas_call(
        functools.partial(kernel, nz),
        out_shape=(
            jax.ShapeDtypeStruct((count, out_cols), BF16),
            jax.ShapeDtypeStruct(outer_params.shape, F32),
            jax.ShapeDtypeStruct(momentum.shape, F32),
            jax.ShapeDtypeStruct(local_params.shape, BF16),
        ),
        in_specs=[smem, smem, smem, pl.BlockSpec(memory_space=pltpu.VMEM)] + [hbm] * 6,
        out_specs=(hbm,) * 4,
        scratch_shapes=scratch,
        compiler_params=pltpu.CompilerParams(
            collective_id=0, has_side_effects=True, vmem_limit_bytes=60 * 2**20
        ),
        cost_estimate=pl.CostEstimate(
            flops=2 * count * depth * out_cols, bytes_accessed=8 * 2**20, transcendentals=count
        ),
    )(scales, rates, slot, gain, tokens, kv_weight, codes, outer_params, momentum, local_params)
    return pl.pallas_call(
        place,
        out_shape=tuple(jax.ShapeDtypeStruct(r.shape, r.dtype) for r in results),
        in_specs=[hbm] * len(results),
        out_specs=(hbm,) * len(results),
        scratch_shapes=[pltpu.VMEM(r.shape, r.dtype) for r in results]
        + [dma((len(results),))] * 2,
        compiler_params=pltpu.CompilerParams(vmem_limit_bytes=60 * 2**20),
    )(*results)


def solution(mesh):
    return jax.shard_map(
        shards,
        mesh=mesh,
        in_specs=(
            P("rep", None, "fsdp", None),
            P("rep", None, "fsdp"),
            P(None, "fsdp", "rep"),
            P(None, "fsdp", "rep"),
            P("rep", None, "fsdp", None),
            P(),
            P(),
            P(("rep", "fsdp"), None),
            P("rep", "fsdp"),
            P("rep", "fsdp", None),
        ),
        out_specs=(
            P(("rep", "fsdp"), None),
            P(None, "fsdp", "rep"),
            P(None, "fsdp", "rep"),
            P("rep", None, "fsdp", None),
        ),
        check_vma=False,
    )
```

```python
import functools

import jax
import jax.numpy as jnp
from jax import lax
from jax.experimental import pallas as pl
from jax.experimental.pallas import tpu as pltpu
from jax.sharding import PartitionSpec as P

F32 = jnp.float32
BF16 = jnp.bfloat16
CHUNKS = 4
NX = 4


def remote(src, dst, send, recv, device):
    return pltpu.make_async_remote_copy(
        src_ref=src,
        dst_ref=dst,
        send_sem=send,
        recv_sem=recv,
        device_id=device,
        device_id_type=pl.DeviceIdType.MESH,
    )


def kernel(
    nz,
    scales,
    rates,
    slot,
    gain,
    tokens,
    weight,
    codes,
    params,
    moment,
    local,
    keyvals_out,
    outer_out,
    moment_out,
    blended_out,
    tok,
    xs,
    relay,
    wraw,
    wk,
    own,
    held,
    c2_send,
    c2_recv,
    c1_send,
    c1_recv,
    kv,
    cb,
    stage_far,
    stage_own,
    fs,
    fr,
    msg,
    rb,
    total,
    pm,
    res,
    rc,
    blocks,
    lp,
    bl,
    load_sem,
    tok_sem,
    wload_sem,
    out_sem,
    xs_send,
    xs_recv,
    rl_send,
    rl_recv,
    fw_send,
    wy_send,
    wy_recv,
    wc_send,
    wc_recv,
    wf_send,
    wf_recv,
    c2s,
    c2r,
    c1s,
    c1r,
    za_send,
    za_recv,
    zb_send,
    zb_recv,
    ph_send,
    ph_recv,
    fb_send,
    fb_recv,
    here,
):
    count = tokens.shape[0]
    width = tokens.shape[1] // 8
    cols = res.shape[3]
    wide = msg.shape[2]
    runs = [(g, g * wide, min(wide, cols - g * wide)) for g in range(4) if g * wide < cols]
    part = kv.shape[1] // CHUNKS
    shard = weight.shape[1]

    me_r = lax.axis_index("rep")
    me_f = lax.axis_index("fsdp")
    z, yh = lax.rem(me_r, nz), lax.div(me_r, nz)
    core, x, y = lax.rem(me_f, 2), lax.rem(lax.div(me_f, 2), NX), lax.div(me_f, 2 * NX)

    def on_x(step):
        return (me_r, y * (2 * NX) + lax.rem(x + step, NX) * 2 + core)

    right, left = on_x(1), on_x(NX - 1)
    across = (me_r, (1 - y) * (2 * NX) + x * 2 + core)
    twin = (me_r, me_f + 1 - 2 * core)
    far = (lax.rem(me_r + nz, 2 * nz), me_f)

    def on_z(k):
        return (yh * nz + lax.rem(z + k, nz), me_f)

    def signal(sem, device):
        pl.semaphore_signal(sem, inc=1, device_id=device, device_id_type=pl.DeviceIdType.MESH)

    barrier = pltpu.get_barrier_semaphore()
    neighbours = (right, left, across, twin, far, on_z(1), on_z(nz - 1))
    for device in neighbours:
        signal(barrier, device)

    def piece(owner, rel):
        h = y if rel == 0 else 1 - y
        start = pl.multiple_of((h * NX + owner) * width, 128)
        return tokens.at[:, pl.ds(start, width)]

    load_codes = pltpu.make_async_copy(codes.at[0], cb, load_sem.at[0])
    wloads = [
        pltpu.make_async_copy(
            weight.at[0, :, pl.ds(n * part, part)], wraw.at[n], wload_sem.at[n]
        )
        for n in range(CHUNKS)
    ]
    load_tok = [
        [
            pltpu.make_async_copy(
                piece(lax.rem(x + d, NX), rel),
                tok.at[rel, d] if d else xs.at[rel, 0],
                tok_sem.at[rel, d],
            )
            for d in range(NX)
        ]
        for rel in range(2)
    ]
    load_pm = [
        pltpu.make_async_copy(ref, pm.at[i], load_sem.at[4 + i])
        for i, ref in enumerate((params, moment))
    ]
    load_lp = pltpu.make_async_copy(local.at[0], lp, load_sem.at[6])
    load_tok[0][2].start()
    load_tok[1][2].start()
    load_codes.start()
    for copy in wloads:
        copy.start()
    for rel, d in ((0, 1), (0, 3), (1, 1), (1, 3), (0, 0), (1, 0)):
        load_tok[rel][d].start()
    for copy in load_pm + [load_lp]:
        copy.start()
    for stage in (stage_far, stage_own):
        stage[...] = jnp.zeros(stage.shape, F32)

    load_codes.wait()
    row_at = lax.broadcasted_iota(jnp.int32, (2, 1), 0)

    def terms(stage, half_y):
        for l in range(2):
            row_scale = jnp.where(row_at == 0, scales[0, l, 0], scales[0, l, 1])
            for to in range(nz):
                for g, start, size in runs:
                    at = pl.multiple_of((half_y * nz + to) * cols + start, 128)
                    row = g * 4 + l * 2
                    stage[to, row : row + 2, :size] = (
                        cb[l, :, pl.ds(at, size)].astype(F32) * row_scale
                    )

    terms(stage_far, 1 - yh)
    for to in range(nz):
        fs[to] = stage_far[to].astype(BF16)
    halves = remote(fs, fr, ph_send.at[0], ph_recv.at[0], far)

    pl.semaphore_wait(barrier, len(neighbours))
    halves.start()

    def tell(turn):
        if 2 ** (turn + 1) < nz:
            for step in (2**turn, nz - 2**turn):
                signal(here.at[turn], on_z(step))

    def learn(turn):
        if 2 ** (turn + 1) < nz:
            pl.semaphore_wait(here.at[turn], 2)

    tell(0)

    relays = [
        remote(tok.at[0, 2], relay.at[0], rl_send.at[0], rl_recv.at[0], right),
        remote(tok.at[1, 2], relay.at[1], rl_send.at[1], rl_recv.at[1], left),
    ]
    forwards = [
        remote(relay.at[0], xs.at[0, 2], fw_send.at[0], xs_recv.at[0, 2], right),
        remote(relay.at[1], xs.at[1, 2], fw_send.at[1], xs_recv.at[1, 2], left),
    ]
    directs = [
        [
            remote(
                tok.at[rel, d],
                xs.at[rel, NX - d],
                xs_send.at[rel, NX - d],
                xs_recv.at[rel, NX - d],
                device,
            )
            for d, device in ((1, right), (3, left))
        ]
        for rel in range(2)
    ]
    for rel in range(2):
        load_tok[rel][2].wait()
        relays[rel].start()
    at_row = lax.broadcasted_iota(jnp.int32, (shard, shard), 0)
    at_col = lax.broadcasted_iota(jnp.int32, (shard, shard), 1)
    gain_col = jnp.sum(
        jnp.where(at_row == at_col, gain[...].astype(F32), 0.0), axis=1, keepdims=True
    )
    w_across = [
        remote(wk.at[n, 0, core], wk.at[n, 1, core], wy_send.at[n], wy_recv.at[n], across)
        for n in range(CHUNKS)
    ]
    w_twin = [
        remote(wk.at[n, 0, core], wk.at[n, 0, core], wc_send.at[n], wc_recv.at[n], twin)
        for n in range(CHUNKS)
    ]
    w_forward = [
        remote(wk.at[n, 1, core], wk.at[n, 1, core], wf_send.at[n], wf_recv.at[n], twin)
        for n in range(CHUNKS)
    ]

    def scale_chunk(n):
        wloads[n].wait()
        wk[n, 0, core] = (wraw[n].astype(F32) * gain_col).astype(BF16)
        w_across[n].start()
        w_twin[n].start()

    def send_direct(rel):
        for i, d in enumerate((1, 3)):
            load_tok[rel][d].wait()
            directs[rel][i].start()

    scale_chunk(0)
    learn(0)
    tell(1)
    send_direct(0)
    scale_chunk(1)
    learn(1)
    tell(2)
    terms(stage_own, yh)

    halves.wait_recv()
    for to in range(nz):
        stage_own[to] = stage_own[to] + fr[to].astype(F32)
        msg[to] = stage_own[to].astype(BF16)
    learn(2)

    def offset(i):
        return nz // 2 + (1 - 2 * lax.rem(i, 2)) * lax.div(i + 1, 2)

    def z_terms(k):
        return remote(msg.at[lax.rem(z + k, nz)], rb.at[k], za_send.at[k], za_recv.at[k], on_z(k))

    def send_terms(i, carry):
        z_terms(offset(i)).start()
        return carry

    lax.fori_loop(0, nz - 1, send_terms, 0)
    scale_chunk(2)
    scale_chunk(3)
    for rel in range(2):
        relays[rel].wait_recv()
        forwards[rel].start()
    send_direct(1)
    directs = directs[0] + directs[1]

    squares = jnp.zeros((count, 1), F32)
    for rel in range(2):
        load_tok[rel][0].wait()
        for d in range(NX):
            block = (tok[rel, d] if d else xs[rel, 0]).astype(F32)
            squares += jnp.sum(block * block, axis=1, keepdims=True)
    inverse = lax.rsqrt(squares / tokens.shape[1] + 1e-05)

    def pass_on(n):
        w_across[n].wait_recv()
        w_forward[n].start()

    def add_terms(k, total):
        z_terms(k).wait_recv()
        return total + rb[k].astype(F32)

    total[...] = lax.fori_loop(1, nz, add_terms, stage_own[z]) / (2 * nz)
    for copy in load_pm:
        copy.wait()
    rate = rates[slot[0]]
    for l in range(2):
        for g, start, size in runs:
            row = g * 4 + l * 2
            at = slice(start, start + size)
            mean_delta = total[row : row + 2, :size]
            new_moment = 0.9 * pm[1, l, :, at] + mean_delta
            new_outer = pm[0, l, :, at] - rate * (mean_delta + 0.9 * new_moment)
            res[0, l, :, at] = new_outer
            res[1, l, :, at] = new_moment
            total[row : row + 2, :size] = new_outer
    rc[yh, z] = total[...].astype(BF16)

    def z_outer(k, source):
        block = rc.at[yh, source]
        return remote(block, block, zb_send.at[k], zb_recv.at[source], on_z(k))

    def send_outer(i, carry):
        z_outer(offset(i), z).start()
        return carry

    lax.fori_loop(0, nz - 1, send_outer, 0)
    outs = [
        pltpu.make_async_copy(res.at[i], ref, out_sem.at[i])
        for i, ref in enumerate((outer_out, moment_out))
    ]
    for copy in outs:
        copy.start()

    pass_on(0)
    pass_on(1)
    pass_on(2)
    for copy in directs + forwards:
        copy.wait_recv()

    sides = (right, left)
    c2 = [
        remote(c2_send.at[n], c2_recv.at[n], c2s.at[n], c2r.at[n], sides[n % 2])
        for n in range(CHUNKS)
    ]
    c1 = [
        [
            remote(c1_send.at[n, s], c1_recv.at[n, s], c1s.at[n, s], c1r.at[n, s], sides[s])
            for s in range(2)
        ]
        for n in range(CHUNKS)
    ]
    rows_of = {0: 1, 1: 3}

    def multiply(n):
        w_twin[n].wait_recv()
        w_forward[n].wait_recv()
        whole = sum(
            jnp.dot(
                xs[rel].reshape(NX * count, width),
                wk[n, rel].reshape(width, part),
                preferred_element_type=F32,
            )
            for rel in range(2)
        )

        def rows(d):
            return whole[d * count : (d + 1) * count]

        via, other = n % 2, 1 - n % 2
        c2_send[n] = rows(2).astype(BF16)
        c2[n].start()
        c1_send[n, other] = rows(rows_of[other]).astype(BF16)
        c1[n][other].start()
        held[n] = rows(rows_of[via])
        own[n] = rows(0)

    def combine(n):
        via = n % 2
        c2[n].wait_recv()
        c1_send[n, via] = (held[n] + c2_recv[n].astype(F32)).astype(BF16)
        c1[n][via].start()

    def finish(n):
        for s in range(2):
            c1[n][s].wait_recv()
        at = n * part
        whole = own[n] + c1_recv[n, 0].astype(F32) + c1_recv[n, 1].astype(F32)
        kv[:, at : at + part] = (whole * inverse).astype(BF16)

    multiply(0)
    multiply(1)
    combine(0)
    multiply(2)
    combine(1)
    combine(2)

    def quarter(turn):
        return lax.rem(lax.div(z, 4) + turn, nz // 4)

    def hand_over(turn):
        block = rc.at[yh, pl.ds(quarter(turn) * 4, 4)]
        return remote(block, block, fb_send.at[turn], fb_recv.at[turn], far)

    for turn in range(nz // 4):
        for i in range(4):
            source = quarter(turn) * 4 + i

            @pl.when(source != z)
            def _():
                z_outer(0, source).wait_recv()

        hand_over(turn).start()
    pass_on(3)
    multiply(3)
    combine(3)

    load_lp.wait()

    def blend(half_y, turn):
        for i in range(4):
            source = quarter(turn) * 4 + i
            blocks[i] = rc[half_y, source].astype(F32)
            for l in range(2):
                for g, start, size in runs:
                    row = g * 4 + l * 2
                    at = pl.ds(pl.multiple_of((half_y * nz + source) * cols + start, 128), size)
                    mine = lp[l, :, at].astype(F32)
                    new = blocks[i, row : row + 2, :size]
                    bl[l, :, at] = (0.5 * mine + 0.5 * new).astype(BF16)

    def write_half(half_y, sem):
        at = pl.ds(pl.multiple_of(half_y * nz * cols, 128), nz * cols)
        copy = pltpu.make_async_copy(bl.at[:, :, at], blended_out.at[0, :, :, at], sem)
        copy.start()
        return copy

    for turn in range(nz // 4):
        blend(yh, turn)
    out_near = write_half(yh, out_sem.at[2])
    for n in range(CHUNKS):
        finish(n)
    out_kv = pltpu.make_async_copy(kv, keyvals_out, out_sem.at[3])
    out_kv.start()
    for turn in range(nz // 4):
        hand_over(turn).wait_recv()
        blend(1 - yh, turn)
    out_far = write_half(1 - yh, out_sem.at[4])


    for copy in relays + directs + forwards + w_across + w_twin + w_forward + [halves] + c2:
        copy.wait_send()
    for turn in range(nz // 4):
        hand_over(turn).wait_send()
    for pair in c1:
        for copy in pair:
            copy.wait_send()

    def drain(k, carry):
        z_terms(k).wait_send()
        z_outer(k, z).wait_send()
        return carry

    lax.fori_loop(1, nz, drain, 0)
    for copy in outs + [out_near, out_far, out_kv]:
        copy.wait()


def place(*refs):
    count = len(refs) // 2
    sems = refs[-1]
    copies = [pltpu.make_async_copy(refs[i], refs[count + i], sems.at[i]) for i in range(count)]
    for copy in copies:
        copy.start()
    for copy in copies:
        copy.wait()


def shards(
    codes, scales, outer_params, momentum, local_params, rates, slot, tokens, gain, kv_weight
):
    nz = lax.axis_size("rep") // 2
    count, depth = tokens.shape
    width = depth // 8
    out_cols = kv_weight.shape[2]
    part = out_cols // CHUNKS
    shard = kv_weight.shape[1]
    full = codes.shape[3]
    cols = outer_params.shape[2]
    wide = (cols // 128 + 3) // 4 * 128
    dma = pltpu.SemaphoreType.DMA
    smem = pl.BlockSpec(memory_space=pltpu.SMEM)
    hbm = pl.BlockSpec(memory_space=pl.ANY)
    scratch = [
        pltpu.VMEM((2, NX, count, width), BF16),
        pltpu.VMEM((2, NX, count, width), BF16),
        pltpu.VMEM((2, count, width), BF16),
        pltpu.VMEM((CHUNKS, shard, part), BF16),
        pltpu.VMEM((CHUNKS, 2, 2, shard, part), BF16),
        pltpu.VMEM((CHUNKS, count, part), F32),
        pltpu.VMEM((CHUNKS, count, part), F32),
        pltpu.VMEM((CHUNKS, count, part), BF16),
        pltpu.VMEM((CHUNKS, count, part), BF16),
        pltpu.VMEM((CHUNKS, 2, count, part), BF16),
        pltpu.VMEM((CHUNKS, 2, count, part), BF16),
        pltpu.VMEM((count, out_cols), BF16),
        pltpu.VMEM((2, 2, full), jnp.int32),
        pltpu.VMEM((nz, 16, wide), F32),
        pltpu.VMEM((nz, 16, wide), F32),
        pltpu.VMEM((nz, 16, wide), BF16),
        pltpu.VMEM((nz, 16, wide), BF16),
        pltpu.VMEM((nz, 16, wide), BF16),
        pltpu.VMEM((nz, 16, wide), BF16),
        pltpu.VMEM((16, wide), F32),
        pltpu.VMEM((2, 2, 2, cols), F32),
        pltpu.VMEM((2, 2, 2, cols), F32),
        pltpu.VMEM((2, nz, 16, wide), BF16),
        pltpu.VMEM((4, 16, wide), F32),
        pltpu.VMEM((2, 2, full), BF16),
        pltpu.VMEM((2, 2, full), BF16),
        dma((7,)),
        dma((2, NX)),
        dma((CHUNKS,)),
        dma((5,)),
        dma((2, NX)),
        dma((2, NX)),
        dma((2,)),
        dma((2,)),
        dma((2,)),
        dma((CHUNKS,)),
        dma((CHUNKS,)),
        dma((CHUNKS,)),
        dma((CHUNKS,)),
        dma((CHUNKS,)),
        dma((CHUNKS,)),
        dma((CHUNKS,)),
        dma((CHUNKS,)),
        dma((CHUNKS, 2)),
        dma((CHUNKS, 2)),
        dma((nz,)),
        dma((nz,)),
        dma((nz,)),
        dma((nz,)),
        dma((1,)),
        dma((1,)),
        dma((4,)),
        dma((4,)),
        pltpu.SemaphoreType.REGULAR((4,)),
    ]
    results = pl.pallas_call(
        functools.partial(kernel, nz),
        out_shape=(
            pltpu.VMEM((count, out_cols), BF16),
            pltpu.VMEM(outer_params.shape, F32),
            pltpu.VMEM(momentum.shape, F32),
            pltpu.VMEM(local_params.shape, BF16),
        ),
        in_specs=[smem, smem, smem, pl.BlockSpec(memory_space=pltpu.VMEM)] + [hbm] * 6,
        out_specs=(pl.BlockSpec(memory_space=pltpu.VMEM),) * 4,
        scratch_shapes=scratch,
        compiler_params=pltpu.CompilerParams(
            collective_id=0, has_side_effects=True, vmem_limit_bytes=60 * 2**20
        ),
        cost_estimate=pl.CostEstimate(
            flops=2 * count * depth * out_cols, bytes_accessed=8 * 2**20, transcendentals=count
        ),
    )(scales, rates, slot, gain, tokens, kv_weight, codes, outer_params, momentum, local_params)
    return pl.pallas_call(
        place,
        out_shape=tuple(jax.ShapeDtypeStruct(r.shape, r.dtype) for r in results),
        in_specs=[pl.BlockSpec(memory_space=pltpu.VMEM)] * len(results),
        out_specs=(hbm,) * len(results),
        scratch_shapes=[dma((len(results),))],
        compiler_params=pltpu.CompilerParams(vmem_limit_bytes=8 * 2**20),
    )(*results)


def solution(mesh):
    return jax.shard_map(
        shards,
        mesh=mesh,
        in_specs=(
            P("rep", None, "fsdp", None),
            P("rep", None, "fsdp"),
            P(None, "fsdp", "rep"),
            P(None, "fsdp", "rep"),
            P("rep", None, "fsdp", None),
            P(),
            P(),
            P(("rep", "fsdp"), None),
            P("rep", "fsdp"),
            P("rep", "fsdp", None),
        ),
        out_specs=(
            P(("rep", "fsdp"), None),
            P(None, "fsdp", "rep"),
            P(None, "fsdp", "rep"),
            P("rep", None, "fsdp", None),
        ),
        check_vma=False,
    )
```

```python
import functools

import jax
import jax.numpy as jnp
from jax import lax
from jax.experimental import pallas as pl
from jax.experimental.pallas import tpu as pltpu
from jax.sharding import PartitionSpec as P

F32 = jnp.float32
BF16 = jnp.bfloat16
CHUNKS = 4
NX = 4


def remote(src, dst, send, recv, device):
    return pltpu.make_async_remote_copy(
        src_ref=src,
        dst_ref=dst,
        send_sem=send,
        recv_sem=recv,
        device_id=device,
        device_id_type=pl.DeviceIdType.MESH,
    )


def kernel(
    nz,
    scales,
    rates,
    slot,
    gain,
    tokens,
    weight,
    codes,
    params,
    moment,
    local,
    keyvals_out,
    outer_out,
    moment_out,
    blended_out,
    tok,
    xs,
    relay,
    wraw,
    wk,
    own,
    held,
    c2_send,
    c2_recv,
    c1_send,
    c1_recv,
    kv,
    cb,
    stage_far,
    stage_own,
    fs,
    fr,
    msg,
    rb,
    total,
    pm,
    res,
    rc,
    blocks,
    lp,
    bl,
    load_sem,
    tok_sem,
    wload_sem,
    out_sem,
    xs_send,
    xs_recv,
    rl_send,
    rl_recv,
    fw_send,
    wy_send,
    wy_recv,
    wc_send,
    wc_recv,
    wf_send,
    wf_recv,
    c2s,
    c2r,
    c1s,
    c1r,
    za_send,
    za_recv,
    zb_send,
    zb_recv,
    ph_send,
    ph_recv,
    fb_send,
    fb_recv,
    here,
):
    count = tokens.shape[0]
    width = tokens.shape[1] // 8
    cols = res.shape[3]
    wide = msg.shape[2]
    runs = [(g, g * wide, min(wide, cols - g * wide)) for g in range(4) if g * wide < cols]
    part = kv.shape[1] // CHUNKS
    shard = weight.shape[1]

    me_r = lax.axis_index("rep")
    me_f = lax.axis_index("fsdp")
    z, yh = lax.rem(me_r, nz), lax.div(me_r, nz)
    core, x, y = lax.rem(me_f, 2), lax.rem(lax.div(me_f, 2), NX), lax.div(me_f, 2 * NX)

    def on_x(step):
        return (me_r, y * (2 * NX) + lax.rem(x + step, NX) * 2 + core)

    right, left = on_x(1), on_x(NX - 1)
    across = (me_r, (1 - y) * (2 * NX) + x * 2 + core)
    twin = (me_r, me_f + 1 - 2 * core)
    far = (lax.rem(me_r + nz, 2 * nz), me_f)

    def on_z(k):
        return (yh * nz + lax.rem(z + k, nz), me_f)

    def signal(sem, device):
        pl.semaphore_signal(sem, inc=1, device_id=device, device_id_type=pl.DeviceIdType.MESH)

    barrier = pltpu.get_barrier_semaphore()
    neighbours = (right, left, across, twin, far, on_z(1), on_z(nz - 1))
    for device in neighbours:
        signal(barrier, device)

    def piece(owner, rel):
        h = y if rel == 0 else 1 - y
        start = pl.multiple_of((h * NX + owner) * width, 128)
        return tokens.at[:, pl.ds(start, width)]

    load_codes = pltpu.make_async_copy(codes.at[0], cb, load_sem.at[0])
    wloads = [
        pltpu.make_async_copy(
            weight.at[0, :, pl.ds(n * part, part)], wraw.at[n], wload_sem.at[n]
        )
        for n in range(CHUNKS)
    ]
    load_tok = [
        [
            pltpu.make_async_copy(
                piece(lax.rem(x + d, NX), rel),
                tok.at[rel, d] if d else xs.at[rel, 0],
                tok_sem.at[rel, d],
            )
            for d in range(NX)
        ]
        for rel in range(2)
    ]
    load_pm = [
        pltpu.make_async_copy(ref, pm.at[i], load_sem.at[4 + i])
        for i, ref in enumerate((params, moment))
    ]
    load_lp = pltpu.make_async_copy(local.at[0], lp, load_sem.at[6])
    load_tok[0][2].start()
    load_tok[1][2].start()
    load_codes.start()
    for copy in wloads:
        copy.start()
    for rel, d in ((0, 1), (0, 3), (1, 1), (1, 3), (0, 0), (1, 0)):
        load_tok[rel][d].start()
    for copy in load_pm + [load_lp]:
        copy.start()
    for stage in (stage_far, stage_own):
        stage[...] = jnp.zeros(stage.shape, F32)

    load_codes.wait()
    row_at = lax.broadcasted_iota(jnp.int32, (2, 1), 0)

    def terms(stage, half_y):
        for l in range(2):
            row_scale = jnp.where(row_at == 0, scales[0, l, 0], scales[0, l, 1])
            for to in range(nz):
                for g, start, size in runs:
                    at = pl.multiple_of((half_y * nz + to) * cols + start, 128)
                    row = g * 4 + l * 2
                    stage[to, row : row + 2, :size] = (
                        cb[l, :, pl.ds(at, size)].astype(F32) * row_scale
                    )

    terms(stage_far, 1 - yh)
    for to in range(nz):
        fs[to] = stage_far[to].astype(BF16)
    halves = remote(fs, fr, ph_send.at[0], ph_recv.at[0], far)

    pl.semaphore_wait(barrier, len(neighbours))
    halves.start()

    def tell(turn):
        if 2 ** (turn + 1) < nz:
            for step in (2**turn, nz - 2**turn):
                signal(here.at[turn], on_z(step))

    def learn(turn):
        if 2 ** (turn + 1) < nz:
            pl.semaphore_wait(here.at[turn], 2)

    tell(0)

    relays = [
        remote(tok.at[0, 2], relay.at[0], rl_send.at[0], rl_recv.at[0], right),
        remote(tok.at[1, 2], relay.at[1], rl_send.at[1], rl_recv.at[1], left),
    ]
    forwards = [
        remote(relay.at[0], xs.at[0, 2], fw_send.at[0], xs_recv.at[0, 2], right),
        remote(relay.at[1], xs.at[1, 2], fw_send.at[1], xs_recv.at[1, 2], left),
    ]
    directs = [
        [
            remote(
                tok.at[rel, d],
                xs.at[rel, NX - d],
                xs_send.at[rel, NX - d],
                xs_recv.at[rel, NX - d],
                device,
            )
            for d, device in ((1, right), (3, left))
        ]
        for rel in range(2)
    ]
    for rel in range(2):
        load_tok[rel][2].wait()
        relays[rel].start()
    at_row = lax.broadcasted_iota(jnp.int32, (shard, shard), 0)
    at_col = lax.broadcasted_iota(jnp.int32, (shard, shard), 1)
    gain_col = jnp.sum(
        jnp.where(at_row == at_col, gain[...].astype(F32), 0.0), axis=1, keepdims=True
    )
    w_across = [
        remote(wk.at[n, 0, core], wk.at[n, 1, core], wy_send.at[n], wy_recv.at[n], across)
        for n in range(CHUNKS)
    ]
    w_twin = [
        remote(wk.at[n, 0, core], wk.at[n, 0, core], wc_send.at[n], wc_recv.at[n], twin)
        for n in range(CHUNKS)
    ]
    w_forward = [
        remote(wk.at[n, 1, core], wk.at[n, 1, core], wf_send.at[n], wf_recv.at[n], twin)
        for n in range(CHUNKS)
    ]

    def scale_chunk(n):
        wloads[n].wait()
        wk[n, 0, core] = (wraw[n].astype(F32) * gain_col).astype(BF16)
        w_across[n].start()
        w_twin[n].start()

    def send_direct(rel):
        for i, d in enumerate((1, 3)):
            load_tok[rel][d].wait()
            directs[rel][i].start()

    scale_chunk(0)
    learn(0)
    tell(1)
    send_direct(0)
    scale_chunk(1)
    learn(1)
    tell(2)
    terms(stage_own, yh)

    halves.wait_recv()
    for to in range(nz):
        stage_own[to] = stage_own[to] + fr[to].astype(F32)
        msg[to] = stage_own[to].astype(BF16)
    learn(2)

    def offset(i):
        return nz // 2 + (1 - 2 * lax.rem(i, 2)) * lax.div(i + 1, 2)

    def z_terms(k):
        return remote(msg.at[lax.rem(z + k, nz)], rb.at[k], za_send.at[k], za_recv.at[k], on_z(k))

    def send_terms(i, carry):
        z_terms(offset(i)).start()
        return carry

    lax.fori_loop(0, nz - 1, send_terms, 0)
    scale_chunk(2)
    scale_chunk(3)
    for rel in range(2):
        relays[rel].wait_recv()
        forwards[rel].start()
    send_direct(1)
    directs = directs[0] + directs[1]

    squares = jnp.zeros((count, 1), F32)
    for rel in range(2):
        load_tok[rel][0].wait()
        for d in range(NX):
            block = (tok[rel, d] if d else xs[rel, 0]).astype(F32)
            squares += jnp.sum(block * block, axis=1, keepdims=True)
    inverse = lax.rsqrt(squares / tokens.shape[1] + 1e-05)

    def pass_on(n):
        w_across[n].wait_recv()
        w_forward[n].start()

    def add_terms(k, total):
        z_terms(k).wait_recv()
        return total + rb[k].astype(F32)

    total[...] = lax.fori_loop(1, nz, add_terms, stage_own[z]) / (2 * nz)
    for copy in load_pm:
        copy.wait()
    rate = rates[slot[0]]
    for l in range(2):
        for g, start, size in runs:
            row = g * 4 + l * 2
            at = slice(start, start + size)
            mean_delta = total[row : row + 2, :size]
            new_moment = 0.9 * pm[1, l, :, at] + mean_delta
            new_outer = pm[0, l, :, at] - rate * (mean_delta + 0.9 * new_moment)
            res[0, l, :, at] = new_outer
            res[1, l, :, at] = new_moment
            total[row : row + 2, :size] = new_outer
    rc[yh, z] = total[...].astype(BF16)

    def z_outer(k, source):
        block = rc.at[yh, source]
        return remote(block, block, zb_send.at[k], zb_recv.at[source], on_z(k))

    def send_outer(i, carry):
        z_outer(offset(i), z).start()
        return carry

    lax.fori_loop(0, nz - 1, send_outer, 0)
    outs = [
        pltpu.make_async_copy(res.at[i], ref, out_sem.at[i])
        for i, ref in enumerate((outer_out, moment_out))
    ]
    for copy in outs:
        copy.start()

    pass_on(0)
    pass_on(1)
    pass_on(2)
    for copy in directs + forwards:
        copy.wait_recv()

    sides = (right, left)
    c2 = [
        remote(c2_send.at[n], c2_recv.at[n], c2s.at[n], c2r.at[n], sides[n % 2])
        for n in range(CHUNKS)
    ]
    c1 = [
        [
            remote(c1_send.at[n, s], c1_recv.at[n, s], c1s.at[n, s], c1r.at[n, s], sides[s])
            for s in range(2)
        ]
        for n in range(CHUNKS)
    ]
    rows_of = {0: 1, 1: 3}

    def multiply(n):
        w_twin[n].wait_recv()
        w_forward[n].wait_recv()
        whole = sum(
            jnp.dot(
                xs[rel].reshape(NX * count, width),
                wk[n, rel].reshape(width, part),
                preferred_element_type=F32,
            )
            for rel in range(2)
        )

        def rows(d):
            return whole[d * count : (d + 1) * count]

        via, other = n % 2, 1 - n % 2
        c2_send[n] = rows(2).astype(BF16)
        c2[n].start()
        c1_send[n, other] = rows(rows_of[other]).astype(BF16)
        c1[n][other].start()
        held[n] = rows(rows_of[via])
        own[n] = rows(0)

    def combine(n):
        via = n % 2
        c2[n].wait_recv()
        c1_send[n, via] = (held[n] + c2_recv[n].astype(F32)).astype(BF16)
        c1[n][via].start()

    def finish(n):
        for s in range(2):
            c1[n][s].wait_recv()
        at = n * part
        whole = own[n] + c1_recv[n, 0].astype(F32) + c1_recv[n, 1].astype(F32)
        kv[:, at : at + part] = (whole * inverse).astype(BF16)

    multiply(0)
    multiply(1)
    combine(0)
    multiply(2)
    combine(1)
    pass_on(3)
    combine(2)

    def quarter(turn):
        return lax.rem(lax.div(z, 4) + turn, nz // 4)

    def hand_over(turn):
        block = rc.at[yh, pl.ds(quarter(turn) * 4, 4)]
        return remote(block, block, fb_send.at[turn], fb_recv.at[turn], far)

    for turn in range(nz // 4):
        for i in range(4):
            source = quarter(turn) * 4 + i

            @pl.when(source != z)
            def _():
                z_outer(0, source).wait_recv()

        hand_over(turn).start()
    multiply(3)
    combine(3)

    load_lp.wait()

    def blend(half_y, turn):
        for i in range(4):
            source = quarter(turn) * 4 + i
            blocks[i] = rc[half_y, source].astype(F32)
            for l in range(2):
                for g, start, size in runs:
                    row = g * 4 + l * 2
                    at = pl.ds(pl.multiple_of((half_y * nz + source) * cols + start, 128), size)
                    mine = lp[l, :, at].astype(F32)
                    new = blocks[i, row : row + 2, :size]
                    bl[l, :, at] = (0.5 * mine + 0.5 * new).astype(BF16)

    def write_half(half_y, sem):
        at = pl.ds(pl.multiple_of(half_y * nz * cols, 128), nz * cols)
        copy = pltpu.make_async_copy(bl.at[:, :, at], blended_out.at[0, :, :, at], sem)
        copy.start()
        return copy

    for turn in range(nz // 4):
        blend(yh, turn)
    out_near = write_half(yh, out_sem.at[2])
    for n in range(CHUNKS):
        finish(n)
    out_kv = pltpu.make_async_copy(kv, keyvals_out, out_sem.at[3])
    out_kv.start()
    for turn in range(nz // 4):
        hand_over(turn).wait_recv()
        blend(1 - yh, turn)
    out_far = write_half(1 - yh, out_sem.at[4])


    for copy in relays + directs + forwards + w_across + w_twin + w_forward + [halves] + c2:
        copy.wait_send()
    for turn in range(nz // 4):
        hand_over(turn).wait_send()
    for pair in c1:
        for copy in pair:
            copy.wait_send()

    def drain(k, carry):
        z_terms(k).wait_send()
        z_outer(k, z).wait_send()
        return carry

    lax.fori_loop(1, nz, drain, 0)
    for copy in outs + [out_near, out_far, out_kv]:
        copy.wait()


def place(*refs):
    count = len(refs) // 2
    sems = refs[-1]
    copies = [pltpu.make_async_copy(refs[i], refs[count + i], sems.at[i]) for i in range(count)]
    for copy in copies:
        copy.start()
    for copy in copies:
        copy.wait()


def shards(
    codes, scales, outer_params, momentum, local_params, rates, slot, tokens, gain, kv_weight
):
    nz = lax.axis_size("rep") // 2
    count, depth = tokens.shape
    width = depth // 8
    out_cols = kv_weight.shape[2]
    part = out_cols // CHUNKS
    shard = kv_weight.shape[1]
    full = codes.shape[3]
    cols = outer_params.shape[2]
    wide = (cols // 128 + 3) // 4 * 128
    dma = pltpu.SemaphoreType.DMA
    smem = pl.BlockSpec(memory_space=pltpu.SMEM)
    hbm = pl.BlockSpec(memory_space=pl.ANY)
    scratch = [
        pltpu.VMEM((2, NX, count, width), BF16),
        pltpu.VMEM((2, NX, count, width), BF16),
        pltpu.VMEM((2, count, width), BF16),
        pltpu.VMEM((CHUNKS, shard, part), BF16),
        pltpu.VMEM((CHUNKS, 2, 2, shard, part), BF16),
        pltpu.VMEM((CHUNKS, count, part), F32),
        pltpu.VMEM((CHUNKS, count, part), F32),
        pltpu.VMEM((CHUNKS, count, part), BF16),
        pltpu.VMEM((CHUNKS, count, part), BF16),
        pltpu.VMEM((CHUNKS, 2, count, part), BF16),
        pltpu.VMEM((CHUNKS, 2, count, part), BF16),
        pltpu.VMEM((count, out_cols), BF16),
        pltpu.VMEM((2, 2, full), jnp.int32),
        pltpu.VMEM((nz, 16, wide), F32),
        pltpu.VMEM((nz, 16, wide), F32),
        pltpu.VMEM((nz, 16, wide), BF16),
        pltpu.VMEM((nz, 16, wide), BF16),
        pltpu.VMEM((nz, 16, wide), BF16),
        pltpu.VMEM((nz, 16, wide), BF16),
        pltpu.VMEM((16, wide), F32),
        pltpu.VMEM((2, 2, 2, cols), F32),
        pltpu.VMEM((2, 2, 2, cols), F32),
        pltpu.VMEM((2, nz, 16, wide), BF16),
        pltpu.VMEM((4, 16, wide), F32),
        pltpu.VMEM((2, 2, full), BF16),
        pltpu.VMEM((2, 2, full), BF16),
        dma((7,)),
        dma((2, NX)),
        dma((CHUNKS,)),
        dma((5,)),
        dma((2, NX)),
        dma((2, NX)),
        dma((2,)),
        dma((2,)),
        dma((2,)),
        dma((CHUNKS,)),
        dma((CHUNKS,)),
        dma((CHUNKS,)),
        dma((CHUNKS,)),
        dma((CHUNKS,)),
        dma((CHUNKS,)),
        dma((CHUNKS,)),
        dma((CHUNKS,)),
        dma((CHUNKS, 2)),
        dma((CHUNKS, 2)),
        dma((nz,)),
        dma((nz,)),
        dma((nz,)),
        dma((nz,)),
        dma((1,)),
        dma((1,)),
        dma((4,)),
        dma((4,)),
        pltpu.SemaphoreType.REGULAR((4,)),
    ]
    results = pl.pallas_call(
        functools.partial(kernel, nz),
        out_shape=(
            pltpu.VMEM((count, out_cols), BF16),
            pltpu.VMEM(outer_params.shape, F32),
            pltpu.VMEM(momentum.shape, F32),
            pltpu.VMEM(local_params.shape, BF16),
        ),
        in_specs=[smem, smem, smem, pl.BlockSpec(memory_space=pltpu.VMEM)] + [hbm] * 6,
        out_specs=(pl.BlockSpec(memory_space=pltpu.VMEM),) * 4,
        scratch_shapes=scratch,
        compiler_params=pltpu.CompilerParams(
            collective_id=0, has_side_effects=True, vmem_limit_bytes=60 * 2**20
        ),
        cost_estimate=pl.CostEstimate(
            flops=2 * count * depth * out_cols, bytes_accessed=8 * 2**20, transcendentals=count
        ),
    )(scales, rates, slot, gain, tokens, kv_weight, codes, outer_params, momentum, local_params)
    return pl.pallas_call(
        place,
        out_shape=tuple(jax.ShapeDtypeStruct(r.shape, r.dtype) for r in results),
        in_specs=[pl.BlockSpec(memory_space=pltpu.VMEM)] * len(results),
        out_specs=(hbm,) * len(results),
        scratch_shapes=[dma((len(results),))],
        compiler_params=pltpu.CompilerParams(vmem_limit_bytes=8 * 2**20),
    )(*results)


def solution(mesh):
    return jax.shard_map(
        shards,
        mesh=mesh,
        in_specs=(
            P("rep", None, "fsdp", None),
            P("rep", None, "fsdp"),
            P(None, "fsdp", "rep"),
            P(None, "fsdp", "rep"),
            P("rep", None, "fsdp", None),
            P(),
            P(),
            P(("rep", "fsdp"), None),
            P("rep", "fsdp"),
            P("rep", "fsdp", None),
        ),
        out_specs=(
            P(("rep", "fsdp"), None),
            P(None, "fsdp", "rep"),
            P(None, "fsdp", "rep"),
            P("rep", None, "fsdp", None),
        ),
        check_vma=False,
    )
```
